128 devices in a mesh: seq: 32 (over y, x, core), ch: 4 (over z).
Axes of the slice: x: 4, y: 4, z: 4, core: 2. Of those that a mesh axis runs over, the one named last changes fastest.
Arguments:
- tokens: bfloat16 [16384, 4096], P('seq', 'ch'), may hold values from -6 to 6
- w_in: bfloat16 [4096, 3, 2048], P(None, None, 'ch'), may hold values from -0.09375 to 0.09375
- w_out: bfloat16 [2048, 4096], P('ch'), may hold values from -0.125 to 0.125
- spectra: float32 [2, 64, 512, 2048], P(None, 'seq', None, 'ch'), may hold values from -8 to 8
Outputs:
- mixed_out: bfloat16 [16384, 4096], P('seq', 'ch')
The draws below stay inside these ranges and needn't reach their ends.
All inputs are finite; a program needn't handle non-finite values.
Results may differ from the reference program's by a relative error of at most 0.007.
Values may be sent and summed in bfloat16 or wider, within the bound.
A program may use at most 128 MiB of HBM per device.

```python
import jax
import jax.numpy as jnp

D = 4096
C = 2048
TOK_DEV = 512
TOKENS = 16384
N_SEQ = 32


def level_of(rng, extent, split, smallest, largest):
    factor_of = 1.0
    for axis_at, parts in split:
        steps = jax.random.uniform(jax.random.fold_in(jax.random.fold_in(rng, 6), axis_at), (parts,), jnp.float32, smallest / len(split), largest / len(split))
        factor_of = factor_of * jnp.repeat(jnp.exp(steps), extent[axis_at] // parts).reshape((-1,) + (1,) * (len(extent) - 1 - axis_at))
    return factor_of


def centred(rng, extent, spread, bound, shards=(), kind=jnp.bfloat16):
    result = jax.random.normal(rng, extent, jnp.float32) * spread
    if len(shards) > 0:
        result = level_of(rng, extent, shards, -0.22, 0.18) * result
    return jnp.clip(result, min=-bound, max=bound).astype(kind)


def setup_inputs(seed: int = 0) -> dict:
    keys = jax.random.split(jax.random.key(seed), 5)
    tokens = centred(keys[0], (TOKENS, D), 1.0, 6.0, ((0, 32), (1, 4)))
    w_in = centred(keys[1], (D, 3, C), D ** -0.5, 0.09375, ((2, 4),))
    w_out = centred(keys[2], (C, D), C ** -0.5, 0.125, ((0, 4),))
    spectra = centred(keys[3], (2, 2 * N_SEQ, TOK_DEV, C), 1.4, 8.0, ((1, 32), (3, 4)), jnp.float32)
    return {"tokens": tokens, "w_in": w_in, "w_out": w_out, "spectra": spectra}


def reference(tokens, w_in, w_out, spectra):
    projected = jnp.einsum('td,dgc->gtc', tokens.astype(jnp.float32), w_in.astype(jnp.float32)).astype(jnp.bfloat16)
    signal = projected[1].astype(jnp.float32) * projected[2].astype(jnp.float32)
    fft_size = 2 * TOKENS
    filter_real = jnp.transpose(spectra[0], (1, 0, 2)).reshape(fft_size, C)
    filter_imag = jnp.transpose(spectra[1], (1, 0, 2)).reshape(fft_size, C)
    block_width = min(C, 256)
    pieces_out = []
    for first_chan in range(0, C, block_width):
        segment = signal[:, first_chan:first_chan + block_width]
        spectrum = jnp.fft.fft(segment, n=fft_size, axis=0)
        filter_block = filter_real[:, first_chan:first_chan + block_width] + 1j * filter_imag[:, first_chan:first_chan + block_width]
        inverse_rows = jnp.fft.ifft(spectrum * filter_block, axis=0)[:TOKENS]
        pieces_out.append(jnp.real(inverse_rows).astype(jnp.float32))
    convolved = jnp.concatenate(pieces_out, axis=1)
    gated_rows = (projected[0].astype(jnp.float32) * convolved).astype(jnp.bfloat16)
    return jnp.dot(gated_rows, w_out, preferred_element_type=jnp.float32).astype(jnp.bfloat16)
```

```python
import numpy as np

import jax
import jax.numpy as jnp
from jax import lax
from jax.sharding import PartitionSpec as P

bf16 = jnp.bfloat16
f32 = jnp.float32


def tables(blocks, tok, chans):
    total = 2 * blocks * tok
    freq = np.arange(blocks + 1)
    outer = 2 * np.pi * (freq[:, None] * np.arange(blocks)[None, :] % (2 * blocks)) / (2 * blocks)
    eye = np.eye(chans)
    first = np.concatenate([np.kron(np.cos(outer), eye), np.kron(-np.sin(outer), eye)])
    last = np.concatenate([np.kron(np.cos(outer.T), eye), np.kron(-np.sin(outer.T), eye)], axis=1)
    pos = np.arange(tok)
    inner = 2 * np.pi * (pos[:, None] * pos[None, :] % tok) / tok
    c, s = np.cos(inner), np.sin(inner)
    forward = np.block([[c, -s], [s, c]])
    inverse = np.block([[c, s], [-s, c]])
    twist = 2 * np.pi * (freq[:, None] * pos[None, :]) / total
    twist = np.stack([np.cos(twist), np.sin(twist)])[:, :, None, :]
    return (
        first.astype(bf16),
        (last / total).astype(bf16),
        forward.astype(bf16),
        inverse.astype(bf16),
        twist.astype(np.float32),
    )


def mm(a, b):
    return jnp.dot(a, b, preferred_element_type=f32)


def convolve(signal, filt, blocks, tok, chans):
    first, last, forward, inverse, twist = tables(blocks, tok, chans)
    rows = (blocks + 1) * chans
    shape = (blocks + 1, chans, tok)
    part = mm(first, signal.reshape(blocks * chans, tok))
    pr, pi = part[:rows].reshape(shape), part[rows:].reshape(shape)
    tc, ts = twist
    q = jnp.concatenate([pr * tc + pi * ts, pi * tc - pr * ts], axis=2)
    x = mm(q.astype(bf16).reshape(rows, 2 * tok), forward)
    xr, xi = x[:, :tok].reshape(shape), x[:, tok:].reshape(shape)
    hr, hi = filt
    z = jnp.concatenate([xr * hr - xi * hi, xr * hi + xi * hr], axis=2)
    u = mm(z.astype(bf16).reshape(rows, 2 * tok), inverse)
    ur, ui = u[:, :tok].reshape(shape), u[:, tok:].reshape(shape)
    v = jnp.concatenate([ur * tc - ui * ts, ur * ts + ui * tc], axis=0)
    return mm(last, v.astype(bf16).reshape(2 * rows, tok)).astype(bf16).reshape(blocks, chans, tok)


def local(tokens, w_in, w_out, spectra):
    blocks = lax.axis_size("seq")
    pos = lax.axis_index("seq")
    tok = tokens.shape[0]
    width = w_in.shape[2]
    chans = width // blocks
    turned = jnp.swapaxes(spectra.astype(bf16), 2, 3)
    own = 2 * pos + jnp.arange(2)
    turned = jnp.where((own > blocks)[None, :, None, None], turned[..., ::-1], turned)
    turned = lax.all_to_all(turned, "seq", split_axis=2, concat_axis=1, tiled=True).astype(f32)
    low = turned[:, : blocks + 1]
    high = turned[:, blocks + 1 :][:, ::-1]
    zero = jnp.zeros_like(low[0, :1])
    filt = jnp.stack(
        [
            low[0] + jnp.concatenate([zero, high[0], zero]),
            low[1] - jnp.concatenate([zero, high[1], zero]),
        ]
    )
    features = lax.all_gather(tokens, "ch", axis=1, tiled=True)
    projected = jnp.einsum("td,dgc->gtc", features, w_in, preferred_element_type=f32).astype(bf16)
    signal = (projected[1].astype(f32) * projected[2].astype(f32)).astype(bf16).T
    signal = lax.all_to_all(signal.reshape(blocks, chans, tok), "seq", split_axis=0, concat_axis=0, tiled=True)
    conv = convolve(signal, filt, blocks, tok, chans)
    conv = lax.all_to_all(conv, "seq", split_axis=0, concat_axis=0, tiled=True)
    conv = conv.reshape(width, tok).T
    gated = (projected[0].astype(f32) * conv.astype(f32)).astype(bf16)
    partial_out = jnp.dot(gated, w_out, preferred_element_type=f32).astype(bf16)
    return lax.psum_scatter(partial_out, "ch", scatter_dimension=1, tiled=True)


def solution(mesh):
    in_specs = (P("seq", "ch"), P(None, None, "ch"), P("ch", None), P(None, "seq", None, "ch"))
    return jax.shard_map(local, mesh=mesh, in_specs=in_specs, out_specs=P("seq", "ch"), check_vma=False)
```

```python
import functools

import numpy as np

import jax
import jax.numpy as jnp
from jax import lax
from jax.experimental import pallas as pl
from jax.experimental.pallas import tpu as pltpu
from jax.sharding import PartitionSpec as P

bf16 = jnp.bfloat16
f32 = jnp.float32
MESH = pl.DeviceIdType.MESH


def tables(blocks, tok, chans):
    total = 2 * blocks * tok
    freq = np.arange(blocks + 1)
    outer = 2 * np.pi * (freq[:, None] * np.arange(blocks)[None, :] % (2 * blocks)) / (2 * blocks)
    eye = np.eye(chans)
    first = np.concatenate([np.kron(np.cos(outer), eye), np.kron(-np.sin(outer), eye)])
    last = np.concatenate([np.kron(np.cos(outer.T), eye), np.kron(-np.sin(outer.T), eye)], axis=1)
    pos = np.arange(tok)
    inner = 2 * np.pi * (pos[:, None] * pos[None, :] % tok) / tok
    c, s = np.cos(inner), np.sin(inner)
    forward = np.block([[c, -s], [s, c]])
    inverse = np.block([[c, s], [-s, c]])
    twist = 2 * np.pi * (freq[:, None] * pos[None, :]) / total
    twist = np.stack([np.cos(twist), np.sin(twist)])[:, :, None, :]
    return (
        first.astype(bf16),
        (last / total).astype(bf16),
        forward.astype(bf16),
        inverse.astype(bf16),
        twist.astype(np.float32),
    )


def mm(a, b):
    return jnp.dot(a, b, preferred_element_type=f32)


def mm_t(a, b):
    return lax.dot_general(a, b, (((1,), (1,)), ((), ())), preferred_element_type=f32)


def unit(n, flipped=None):
    row = lax.broadcasted_iota(jnp.int32, (n, n), 0)
    col = lax.broadcasted_iota(jnp.int32, (n, n), 1)
    if flipped is not None:
        row = jnp.where(flipped, n - 1 - row, row)
    return jnp.where(row == col, 1.0, 0.0).astype(bf16)


def kernel(
    nz, blocks, tok, chans,
    tokens_hbm, w_in_hbm, w_out_hbm, spectra_hbm, first_hbm, last_hbm, forward_hbm, inverse_hbm, twist_hbm,
    out_ref,
    feat, w_in, w_out, spec, first, last, forward, inverse, twist,
    acc, hsend, hrecv, filt, sig, xrecv, part, q, v, y, conv, qt,
    opp_send, opp_recv, side, side_send, side_recv,
    load_sem, ag_send, ag_recv, h_send, h_recv, s_send, s_recv, c_send, c_recv, r_send, r_recv,
):
    me = lax.axis_index("seq")
    z = lax.axis_index("ch")
    right, left, opp = lax.rem(z + 1, nz), lax.rem(z + nz - 1, nz), lax.rem(z + 2, nz)
    width = chans * blocks
    depth = tokens_hbm.shape[1]
    half = tok // 2
    top, low = pl.ds(0, half), pl.ds(half, half)
    rows = (blocks + 1) * chans

    def load(src, dst, sem):
        return pltpu.make_async_copy(src, dst, load_sem.at[sem])

    def load_w(block, sem):
        at = pl.ds(pl.multiple_of(block * depth, depth), depth)
        return load(w_in_hbm.at[:, at], w_in.at[:, at], sem)

    tok_load = load(tokens_hbm, feat.at[z], 0)
    spec_load = load(spectra_hbm, spec, 1)
    w_loads = [load_w(z, 2), load_w(left, 3), load_w(right, 4), load_w(opp, 5)]
    rest = [
        load(w_out_hbm, w_out, 6), load(first_hbm, first, 7), load(last_hbm, last, 8),
        load(forward_hbm, forward, 9), load(inverse_hbm, inverse, 10), load(twist_hbm, twist, 11),
    ]
    tok_load.start()
    spec_load.start()
    for copy in w_loads + rest:
        copy.start()

    barrier = pltpu.get_barrier_semaphore()
    for near in (left, right):
        pl.semaphore_signal(barrier, inc=1, device_id=(me, near), device_id_type=MESH)

    @pl.loop(1, blocks)
    def _(k):
        pl.semaphore_signal(barrier, inc=1, device_id=(lax.rem(me + k, blocks), z), device_id_type=MESH)

    pl.semaphore_wait(barrier, blocks + 1)
    tok_load.wait()

    def hop(block, at, sem, to):
        return pltpu.make_async_remote_copy(
            src_ref=feat.at[block, at], dst_ref=feat.at[block, at],
            send_sem=ag_send.at[sem], recv_sem=ag_recv.at[sem],
            device_id=(me, to), device_id_type=MESH,
        )

    gather = [hop(z, top, 0, right), hop(z, low, 1, left), hop(z, low, 2, right), hop(z, top, 3, left)]
    for copy in gather:
        copy.start()

    def swap(src, dst, send, recv, peer, entry):
        return pltpu.make_async_remote_copy(
            src_ref=src.at[peer], dst_ref=dst.at[entry],
            send_sem=send.at[peer], recv_sem=recv.at[entry],
            device_id=(peer, z), device_id_type=MESH,
        )

    def swap_start(*refs):
        @pl.loop(1, blocks)
        def _(k):
            swap(*refs, lax.rem(me + k, blocks), me).start()

    def swap_arrived(*refs):
        @pl.loop(1, blocks)
        def _(k):
            peer = lax.rem(me + k, blocks)
            swap(*refs, peer, peer).wait_recv()

    def swap_sent(*refs):
        @pl.loop(1, blocks)
        def _(k):
            swap(*refs, lax.rem(me + k, blocks), me).wait_send()

    h_refs = (hsend, hrecv, h_send, h_recv)
    spec_load.wait()
    for a in range(2):
        for ri in range(2):
            turned = mm_t(unit(width), spec[ri, a].astype(bf16)).astype(bf16)
            turned = mm(turned, unit(tok, 2 * me + a > blocks)).astype(bf16)
            hsend[:, ri, a] = turned.reshape(blocks, chans, tok)
    swap_start(*h_refs)
    hrecv[pl.ds(me, 1)] = hsend[pl.ds(me, 1)]

    def project(block, start, count, fresh=False):
        at = pl.ds(pl.multiple_of(block * depth, depth), depth)

        @pl.loop(0, 3)
        def _(g):
            for r in range(start, start + count, half):
                term = mm(feat[block, r:r + half], w_in[g, at])
                if fresh:
                    acc[g, r:r + half] = term
                else:
                    acc[g, r:r + half] += term

    w_loads[0].wait()
    project(z, 0, tok, True)
    hop(left, top, 0, right).wait_recv()
    far_top = hop(left, top, 4, right)
    far_top.start()
    hop(right, low, 1, left).wait_recv()
    far_low = hop(right, low, 5, left)
    far_low.start()
    w_loads[1].wait()
    w_loads[2].wait()
    project(left, 0, half)
    project(right, half, half)
    hop(left, low, 2, right).wait_recv()
    project(left, half, half)
    hop(right, top, 3, left).wait_recv()
    project(right, 0, half)
    w_loads[3].wait()
    hop(opp, top, 4, right).wait_recv()
    project(opp, 0, half)
    hop(opp, low, 5, left).wait_recv()
    project(opp, half, half)

    s_refs = (sig, xrecv, s_send, s_recv)
    signal = (acc[1].astype(bf16).astype(f32) * acc[2].astype(bf16).astype(f32)).astype(bf16)
    sig[...] = mm_t(unit(width), signal).astype(bf16).reshape(blocks, chans, tok)
    swap_start(*s_refs)
    xrecv[pl.ds(me, 1)] = sig[pl.ds(me, 1)]
    qt[...] = mm_t(unit(width), acc[0].astype(bf16)).astype(bf16)

    swap_arrived(*h_refs)
    filt[:, 0] = hrecv[0, :, 0].astype(f32)
    filt[:, blocks] = hrecv[blocks // 2, :, 0].astype(f32)

    @pl.loop(1, blocks)
    def _(a):
        other = 2 * blocks - a
        near = hrecv[a // 2, :, a % 2].astype(f32)
        far = hrecv[other // 2, :, other % 2].astype(f32)
        filt[0, a] = near[0] + far[0]
        filt[1, a] = near[1] - far[1]

    for copy in rest:
        copy.wait()
    swap_arrived(*s_refs)

    x = xrecv[...].reshape(blocks * chans, tok)
    for i in range(2):
        part[i] = mm(first[i * rows:(i + 1) * rows], x)

    def at(a):
        return pl.ds(pl.multiple_of(a * chans, chans), chans)

    @pl.loop(0, blocks + 1)
    def _(a):
        pr, pi = part[0, at(a)], part[1, at(a)]
        tc, ts = twist[0, a], twist[1, a]
        q[at(a), :tok] = (pr * tc + pi * ts).astype(bf16)
        q[at(a), tok:] = (pi * tc - pr * ts).astype(bf16)

    def inner(table):
        for i in range(2):
            part[i] = mm(q[...], table[:, i * tok:(i + 1) * tok])

    inner(forward)

    @pl.loop(0, blocks + 1)
    def _(a):
        xr, xi = part[0, at(a)], part[1, at(a)]
        hr, hi = filt[0, a], filt[1, a]
        q[at(a), :tok] = (xr * hr - xi * hi).astype(bf16)
        q[at(a), tok:] = (xr * hi + xi * hr).astype(bf16)

    inner(inverse)

    @pl.loop(0, blocks + 1)
    def _(a):
        ur, ui = part[0, at(a)], part[1, at(a)]
        tc, ts = twist[0, a], twist[1, a]
        v[0, at(a)] = (ur * tc - ui * ts).astype(bf16)
        v[1, at(a)] = (ur * ts + ui * tc).astype(bf16)

    c_refs = (y, conv, c_send, c_recv)
    y[...] = mm(last[...], v[...].reshape(2 * rows, tok)).astype(bf16).reshape(blocks, chans, tok)
    swap_start(*c_refs)
    conv[pl.ds(me, 1)] = y[pl.ds(me, 1)]
    swap_arrived(*c_refs)

    gated_t = (qt[...].astype(f32) * conv[...].reshape(width, tok).astype(f32)).astype(bf16)
    gated = mm_t(unit(tok), gated_t).astype(bf16)

    def term(block, start):
        cols = pl.ds(pl.multiple_of(block * depth, depth), depth)
        return mm(gated[start:start + half], w_out[:, cols])

    def give(src, dst, sem, to):
        return pltpu.make_async_remote_copy(
            src_ref=src, dst_ref=dst, send_sem=r_send.at[sem], recv_sem=r_recv.at[sem],
            device_id=(me, to), device_id_type=MESH,
        )

    def opp_give(i, to):
        return give(opp_send.at[i], opp_recv.at[i], i, to)

    def side_give(i, h, to):
        return give(side_send.at[i, h], side_recv.at[i, h], 2 + 2 * i + h, to)

    gives = [
        opp_give(0, right), opp_give(1, left), side_give(0, 1, right), side_give(1, 0, left),
        side_give(0, 0, right), side_give(1, 1, left),
    ]
    opp_send[0] = term(opp, 0).astype(bf16)
    gives[0].start()
    opp_send[1] = term(opp, half).astype(bf16)
    gives[1].start()
    side_send[0, 1] = term(right, half).astype(bf16)
    gives[2].start()
    side_send[1, 0] = term(left, 0).astype(bf16)
    gives[3].start()
    side[0] = term(right, 0)
    side[1] = term(left, half)
    opp_give(0, right).wait_recv()
    side_send[0, 0] = (side[0] + opp_recv[0].astype(f32)).astype(bf16)
    gives[4].start()
    opp_give(1, left).wait_recv()
    side_send[1, 1] = (side[1] + opp_recv[1].astype(f32)).astype(bf16)
    gives[5].start()
    side[0] = term(z, 0)
    side[1] = term(z, half)
    side_give(0, 1, right).wait_recv()
    side_give(1, 0, left).wait_recv()
    side[1] += side_recv[0, 1].astype(f32)
    side[0] += side_recv[1, 0].astype(f32)
    side_give(0, 0, right).wait_recv()
    out_ref[:half] = (side[0] + side_recv[0, 0].astype(f32)).astype(bf16)
    side_give(1, 1, left).wait_recv()
    out_ref[half:] = (side[1] + side_recv[1, 1].astype(f32)).astype(bf16)

    for copy in gather + [far_top, far_low] + gives:
        copy.wait_send()
    swap_sent(*h_refs)
    swap_sent(*s_refs)
    swap_sent(*c_refs)


def local(nz, blocks, tokens, w_in, w_out, spectra):
    tok, depth = tokens.shape
    width = w_in.shape[2]
    chans = width // blocks
    rows = (blocks + 1) * chans
    half = tok // 2
    consts = [jnp.asarray(t) for t in tables(blocks, tok, chans)]
    dma = pltpu.SemaphoreType.DMA
    vmem = pltpu.VMEM
    scratch = [
        vmem((nz, tok, depth), bf16),
        vmem((3, nz * depth, width), bf16),
        vmem(w_out.shape, bf16),
        vmem(spectra.shape, f32),
        *[vmem(t.shape, t.dtype) for t in consts],
        vmem((3, tok, width), f32),
        vmem((blocks, 2, 2, chans, tok), bf16),
        vmem((blocks, 2, 2, chans, tok), bf16),
        vmem((2, blocks + 1, chans, tok), f32),
        vmem((blocks, chans, tok), bf16),
        vmem((blocks, chans, tok), bf16),
        vmem((2, rows, tok), f32),
        vmem((rows, 2 * tok), bf16),
        vmem((2, rows, tok), bf16),
        vmem((blocks, chans, tok), bf16),
        vmem((blocks, chans, tok), bf16),
        vmem((width, tok), bf16),
        vmem((2, half, depth), bf16),
        vmem((2, half, depth), bf16),
        vmem((2, half, depth), f32),
        vmem((2, 2, half, depth), bf16),
        vmem((2, 2, half, depth), bf16),
        dma((12,)),
        dma((6,)), dma((6,)),
        dma((blocks,)), dma((blocks,)),
        dma((blocks,)), dma((blocks,)),
        dma((blocks,)), dma((blocks,)),
        dma((6,)), dma((6,)),
    ]
    return pl.pallas_call(
        functools.partial(kernel, nz, blocks, tok, chans),
        out_shape=jax.ShapeDtypeStruct((tok, depth), bf16),
        in_specs=[pl.BlockSpec(memory_space=pl.ANY)] * 9,
        out_specs=pl.BlockSpec(memory_space=pltpu.VMEM),
        scratch_shapes=scratch,
        compiler_params=pltpu.CompilerParams(
            collective_id=0, has_side_effects=True, vmem_limit_bytes=62 * 1024 * 1024
        ),
    )(tokens, jnp.swapaxes(w_in, 0, 1), w_out, spectra, *consts)


def solution(mesh):
    in_specs = (P("seq", "ch"), P(None, None, "ch"), P("ch", None), P(None, "seq", None, "ch"))
    body = functools.partial(local, mesh.shape["ch"], mesh.shape["seq"])
    return jax.shard_map(body, mesh=mesh, in_specs=in_specs, out_specs=P("seq", "ch"), check_vma=False)
```

```python
import functools

import numpy as np

import jax
import jax.numpy as jnp
from jax import lax
from jax.experimental import pallas as pl
from jax.experimental.pallas import tpu as pltpu
from jax.sharding import PartitionSpec as P

bf16 = jnp.bfloat16
f32 = jnp.float32
MESH = pl.DeviceIdType.MESH


def tables(blocks, tok, chans):
    total = 2 * blocks * tok
    freq = np.arange(blocks + 1)
    outer = 2 * np.pi * (freq[:, None] * np.arange(blocks)[None, :] % (2 * blocks)) / (2 * blocks)
    eye = np.eye(chans)
    first = np.concatenate([np.kron(np.cos(outer), eye), np.kron(-np.sin(outer), eye)])
    last = np.concatenate([np.kron(np.cos(outer.T), eye), np.kron(-np.sin(outer.T), eye)], axis=1)
    pos = np.arange(tok)
    inner = 2 * np.pi * (pos[:, None] * pos[None, :] % tok) / tok
    c, s = np.cos(inner), np.sin(inner)
    forward = np.block([[c, -s], [s, c]])
    inverse = np.block([[c, s], [-s, c]])
    twist = 2 * np.pi * (freq[:, None] * pos[None, :]) / total
    twist = np.stack([np.cos(twist), np.sin(twist)])[:, :, None, :]
    return (
        first.astype(bf16),
        (last / total).astype(bf16),
        forward.astype(bf16),
        inverse.astype(bf16),
        twist.astype(np.float32),
    )


def mm(a, b):
    return jnp.dot(a, b, preferred_element_type=f32)


def mm_t(a, b):
    return lax.dot_general(a, b, (((1,), (1,)), ((), ())), preferred_element_type=f32)


def unit(n, flipped=None):
    row = lax.broadcasted_iota(jnp.int32, (n, n), 0)
    col = lax.broadcasted_iota(jnp.int32, (n, n), 1)
    if flipped is not None:
        row = jnp.where(flipped, n - 1 - row, row)
    return jnp.where(row == col, 1.0, 0.0).astype(bf16)


def kernel(
    nz, blocks, tok, chans,
    tokens_hbm, w_in_hbm, w_out_hbm, spectra_hbm, first_hbm, last_hbm, forward_hbm, inverse_hbm, twist_hbm,
    out_ref,
    feat, w_in, w_cols, w_relay, spec, first, last, forward, inverse, twist,
    acc, hsend, hrecv, filt, sig, xrecv, part, q, v, y, conv, qt,
    gall, side,
    load_sem, ag_send, ag_recv, h_send, h_recv, s_send, s_recv, c_send, c_recv, r_send, r_recv, w_send, w_recv,
):
    me = lax.axis_index("seq")
    z = lax.axis_index("ch")
    right, left, opp = lax.rem(z + 1, nz), lax.rem(z + nz - 1, nz), lax.rem(z + 2, nz)
    width = chans * blocks
    depth = tokens_hbm.shape[1]
    half = tok // 2
    top, low = pl.ds(0, half), pl.ds(half, half)
    rows = (blocks + 1) * chans

    def load(src, dst, sem):
        return pltpu.make_async_copy(src, dst, load_sem.at[sem])

    def load_w(block, sem):
        at = pl.ds(pl.multiple_of(block * depth, depth), depth)
        return load(w_in_hbm.at[:, at], w_in.at[:, at], sem)

    tok_load = load(tokens_hbm, feat.at[z], 0)
    spec_load = load(spectra_hbm, spec, 1)
    w_loads = [load_w(z, 2), load_w(left, 3), load_w(right, 4), load_w(opp, 5)]
    rest = [
        load(first_hbm, first, 7), load(last_hbm, last, 8),
        load(forward_hbm, forward, 9), load(inverse_hbm, inverse, 10), load(twist_hbm, twist, 11),
    ]
    tok_load.start()
    spec_load.start()
    for copy in w_loads + rest:
        copy.start()

    barrier = pltpu.get_barrier_semaphore()
    for near in (left, right):
        pl.semaphore_signal(barrier, inc=1, device_id=(me, near), device_id_type=MESH)

    @pl.loop(1, blocks)
    def _(k):
        pl.semaphore_signal(barrier, inc=1, device_id=(lax.rem(me + k, blocks), z), device_id_type=MESH)

    pl.semaphore_wait(barrier, blocks + 1)
    tok_load.wait()

    core = lax.rem(me, 2)
    sibling = me + 1 - 2 * core
    part_w = width // 2

    def w_rows(c, start=0, count=part_w):
        return pl.ds(pl.multiple_of(c * part_w, part_w) + start, count)

    def w_give(src, dst, sem, to, line=me):
        return pltpu.make_async_remote_copy(
            src_ref=src, dst_ref=dst, send_sem=w_send.at[sem], recv_sem=w_recv.at[sem],
            device_id=(line, to), device_id_type=MESH,
        )

    def w_slice(rows_at, block):
        return w_out_hbm.at[rows_at, pl.ds(pl.multiple_of(block * depth, depth), depth)]

    quarter = part_w // 2
    first_q, second_q = w_rows(core, 0, quarter), w_rows(core, quarter, quarter)
    w_near = [
        w_give(w_slice(first_q, opp), w_relay.at[0], 2, right),
        w_give(w_slice(second_q, opp), w_relay.at[1], 3, left),
        w_give(w_slice(w_rows(core), right), w_cols.at[z, w_rows(core)], 0, right),
        w_give(w_slice(w_rows(core), left), w_cols.at[z, w_rows(core)], 1, left),
    ]
    w_got = [
        w_give(w_relay.at[0], w_relay.at[0], 2, right),
        w_give(w_relay.at[1], w_relay.at[1], 3, left),
        w_give(w_cols.at[left, w_rows(core)], w_cols.at[left, w_rows(core)], 0, right),
        w_give(w_cols.at[right, w_rows(core)], w_cols.at[right, w_rows(core)], 1, left),
    ]
    w_fwd = [
        w_give(w_relay.at[0], w_cols.at[left, first_q], 4, right),
        w_give(w_relay.at[1], w_cols.at[right, second_q], 5, left),
    ]

    def w_shares(c):
        return [
            w_give(w_cols.at[block, w_rows(c)], w_cols.at[block, w_rows(c)], 6 + i, z, sibling)
            for i, block in enumerate((left, right, opp))
        ]

    w_share, w_theirs = w_shares(core), w_shares(1 - core)
    own_w = load(w_slice(pl.ds(0, width), z), w_cols.at[z], 6)
    own_w.start()

    def hop(block, at, sem, to):
        return pltpu.make_async_remote_copy(
            src_ref=feat.at[block, at], dst_ref=feat.at[block, at],
            send_sem=ag_send.at[sem], recv_sem=ag_recv.at[sem],
            device_id=(me, to), device_id_type=MESH,
        )

    gather = [hop(z, top, 0, right), hop(z, low, 1, left), hop(z, low, 2, right), hop(z, top, 3, left)]
    for copy in gather:
        copy.start()

    def swap(src, dst, send, recv, peer, entry):
        return pltpu.make_async_remote_copy(
            src_ref=src.at[peer], dst_ref=dst.at[entry],
            send_sem=send.at[peer], recv_sem=recv.at[entry],
            device_id=(peer, z), device_id_type=MESH,
        )

    def swap_start(*refs):
        @pl.loop(1, blocks)
        def _(k):
            swap(*refs, lax.rem(me + k, blocks), me).start()

    def swap_arrived(*refs):
        @pl.loop(1, blocks)
        def _(k):
            peer = lax.rem(me + k, blocks)
            swap(*refs, peer, peer).wait_recv()

    def swap_sent(*refs):
        @pl.loop(1, blocks)
        def _(k):
            swap(*refs, lax.rem(me + k, blocks), me).wait_send()

    h_refs = (hsend, hrecv, h_send, h_recv)
    spec_load.wait()
    for a in range(2):
        for ri in range(2):
            turned = mm_t(unit(width), spec[ri, a].astype(bf16)).astype(bf16)
            turned = mm(turned, unit(tok, 2 * me + a > blocks)).astype(bf16)
            hsend[:, ri, a] = turned.reshape(blocks, chans, tok)
    swap_start(*h_refs)
    hrecv[pl.ds(me, 1)] = hsend[pl.ds(me, 1)]

    def project(block, start, count, fresh=False):
        at = pl.ds(pl.multiple_of(block * depth, depth), depth)

        @pl.loop(0, 3)
        def _(g):
            for r in range(start, start + count, half):
                term = mm(feat[block, r:r + half], w_in[g, at])
                if fresh:
                    acc[g, r:r + half] = term
                else:
                    acc[g, r:r + half] += term

    w_loads[0].wait()
    project(z, 0, tok, True)
    hop(left, top, 0, right).wait_recv()
    far_top = hop(left, top, 4, right)
    far_top.start()
    hop(right, low, 1, left).wait_recv()
    far_low = hop(right, low, 5, left)
    far_low.start()
    w_loads[1].wait()
    w_loads[2].wait()
    project(left, 0, half)
    project(right, half, half)
    hop(left, low, 2, right).wait_recv()
    project(left, half, half)
    hop(right, top, 3, left).wait_recv()
    project(right, 0, half)
    w_loads[3].wait()
    hop(opp, top, 4, right).wait_recv()
    project(opp, 0, half)
    hop(opp, low, 5, left).wait_recv()
    for copy in w_near:
        copy.start()
    project(opp, half, half)

    s_refs = (sig, xrecv, s_send, s_recv)
    signal = (acc[1].astype(bf16).astype(f32) * acc[2].astype(bf16).astype(f32)).astype(bf16)
    sig[...] = mm_t(unit(width), signal).astype(bf16).reshape(blocks, chans, tok)
    swap_start(*s_refs)
    xrecv[pl.ds(me, 1)] = sig[pl.ds(me, 1)]
    qt[...] = mm_t(unit(width), acc[0].astype(bf16)).astype(bf16)

    swap_arrived(*h_refs)
    filt[:, 0] = hrecv[0, :, 0].astype(f32)
    filt[:, blocks] = hrecv[blocks // 2, :, 0].astype(f32)

    @pl.loop(1, blocks)
    def _(a):
        other = 2 * blocks - a
        near = hrecv[a // 2, :, a % 2].astype(f32)
        far = hrecv[other // 2, :, other % 2].astype(f32)
        filt[0, a] = near[0] + far[0]
        filt[1, a] = near[1] - far[1]

    for copy in rest:
        copy.wait()
    swap_arrived(*s_refs)

    w_got[0].wait_recv()
    w_fwd[0].start()
    w_got[1].wait_recv()
    w_fwd[1].start()

    x = xrecv[...].reshape(blocks * chans, tok)
    for i in range(2):
        part[i] = mm(first[i * rows:(i + 1) * rows], x)

    def at(a):
        return pl.ds(pl.multiple_of(a * chans, chans), chans)

    @pl.loop(0, blocks + 1)
    def _(a):
        pr, pi = part[0, at(a)], part[1, at(a)]
        tc, ts = twist[0, a], twist[1, a]
        q[at(a), :tok] = (pr * tc + pi * ts).astype(bf16)
        q[at(a), tok:] = (pi * tc - pr * ts).astype(bf16)

    def inner(table):
        for i in range(2):
            part[i] = mm(q[...], table[:, i * tok:(i + 1) * tok])

    inner(forward)

    @pl.loop(0, blocks + 1)
    def _(a):
        xr, xi = part[0, at(a)], part[1, at(a)]
        hr, hi = filt[0, a], filt[1, a]
        q[at(a), :tok] = (xr * hr - xi * hi).astype(bf16)
        q[at(a), tok:] = (xr * hi + xi * hr).astype(bf16)

    inner(inverse)

    @pl.loop(0, blocks + 1)
    def _(a):
        ur, ui = part[0, at(a)], part[1, at(a)]
        tc, ts = twist[0, a], twist[1, a]
        v[0, at(a)] = (ur * tc - ui * ts).astype(bf16)
        v[1, at(a)] = (ur * ts + ui * tc).astype(bf16)

    c_refs = (y, conv, c_send, c_recv)
    y[...] = mm(last[...], v[...].reshape(2 * rows, tok)).astype(bf16).reshape(blocks, chans, tok)
    swap_start(*c_refs)
    conv[pl.ds(me, 1)] = y[pl.ds(me, 1)]
    w_got[2].wait_recv()
    w_share[0].start()
    w_got[3].wait_recv()
    w_share[1].start()
    swap_arrived(*c_refs)

    gated_t = (qt[...].astype(f32) * conv[...].reshape(width, tok).astype(f32)).astype(bf16)
    gall[pl.ds(z, 1)] = mm_t(unit(tok), gated_t).astype(bf16)[None]

    def ghop(block, at, sem, to):
        return pltpu.make_async_remote_copy(
            src_ref=gall.at[block, at], dst_ref=gall.at[block, at],
            send_sem=r_send.at[sem], recv_sem=r_recv.at[sem],
            device_id=(me, to), device_id_type=MESH,
        )

    gives = [ghop(z, top, 0, right), ghop(z, low, 1, left), ghop(z, low, 2, right), ghop(z, top, 3, left)]
    for copy in gives:
        copy.start()

    def term(block, h):
        return mm(gall[block, h * half:(h + 1) * half], w_cols[block])

    w_fwd[0].wait_recv()
    w_fwd[1].wait_recv()
    w_share[2].start()
    own_w.wait()
    side[0] = term(z, 0)
    side[1] = term(z, 1)
    ghop(left, top, 0, right).wait_recv()
    far_gtop = ghop(left, top, 4, right)
    far_gtop.start()
    ghop(right, low, 1, left).wait_recv()
    far_glow = ghop(right, low, 5, left)
    far_glow.start()
    w_theirs[0].wait_recv()
    w_theirs[1].wait_recv()
    side[0] += term(left, 0)
    side[1] += term(right, 1)
    ghop(left, low, 2, right).wait_recv()
    side[1] += term(left, 1)
    ghop(right, top, 3, left).wait_recv()
    side[0] += term(right, 0)
    w_theirs[2].wait_recv()
    ghop(opp, top, 4, right).wait_recv()
    out_ref[:half] = (side[0] + term(opp, 0)).astype(bf16)
    ghop(opp, low, 5, left).wait_recv()
    out_ref[half:] = (side[1] + term(opp, 1)).astype(bf16)

    gives += [far_gtop, far_glow] + w_near + w_fwd + w_share
    for copy in gather + [far_top, far_low] + gives:
        copy.wait_send()
    swap_sent(*h_refs)
    swap_sent(*s_refs)
    swap_sent(*c_refs)


def local(nz, blocks, tokens, w_in, w_out, spectra):
    tok, depth = tokens.shape
    width = w_in.shape[2]
    chans = width // blocks
    rows = (blocks + 1) * chans
    half = tok // 2
    consts = [jnp.asarray(t) for t in tables(blocks, tok, chans)]
    dma = pltpu.SemaphoreType.DMA
    vmem = pltpu.VMEM
    scratch = [
        vmem((nz, tok, depth), bf16),
        vmem((3, nz * depth, width), bf16),
        vmem((nz, width, depth), bf16),
        vmem((2, width // 4, depth), bf16),
        vmem(spectra.shape, f32),
        *[vmem(t.shape, t.dtype) for t in consts],
        vmem((3, tok, width), f32),
        vmem((blocks, 2, 2, chans, tok), bf16),
        vmem((blocks, 2, 2, chans, tok), bf16),
        vmem((2, blocks + 1, chans, tok), f32),
        vmem((blocks, chans, tok), bf16),
        vmem((blocks, chans, tok), bf16),
        vmem((2, rows, tok), f32),
        vmem((rows, 2 * tok), bf16),
        vmem((2, rows, tok), bf16),
        vmem((blocks, chans, tok), bf16),
        vmem((blocks, chans, tok), bf16),
        vmem((width, tok), bf16),
        vmem((nz, tok, width), bf16),
        vmem((2, half, depth), f32),
        dma((12,)),
        dma((6,)), dma((6,)),
        dma((blocks,)), dma((blocks,)),
        dma((blocks,)), dma((blocks,)),
        dma((blocks,)), dma((blocks,)),
        dma((6,)), dma((6,)),
        dma((9,)), dma((9,)),
    ]
    return pl.pallas_call(
        functools.partial(kernel, nz, blocks, tok, chans),
        out_shape=jax.ShapeDtypeStruct((tok, depth), bf16),
        in_specs=[pl.BlockSpec(memory_space=pl.ANY)] * 9,
        out_specs=pl.BlockSpec(memory_space=pltpu.VMEM),
        scratch_shapes=scratch,
        compiler_params=pltpu.CompilerParams(
            collective_id=0, has_side_effects=True, vmem_limit_bytes=62 * 1024 * 1024
        ),
    )(tokens, jnp.swapaxes(w_in, 0, 1), w_out, spectra, *consts)


def solution(mesh):
    in_specs = (P("seq", "ch"), P(None, None, "ch"), P("ch", None), P(None, "seq", None, "ch"))
    body = functools.partial(local, mesh.shape["ch"], mesh.shape["seq"])
    return jax.shard_map(body, mesh=mesh, in_specs=in_specs, out_specs=P("seq", "ch"), check_vma=False)
```

```python
import functools

import numpy as np

import jax
import jax.numpy as jnp
from jax import lax
from jax.experimental import pallas as pl
from jax.experimental.pallas import tpu as pltpu
from jax.sharding import PartitionSpec as P

bf16 = jnp.bfloat16
f32 = jnp.float32
MESH = pl.DeviceIdType.MESH
IN_PARTS = (2, 2)
OUT_PARTS = (1, 1, 2)


def spans(parts, tok):
    ends = np.cumsum((0,) + parts) * (tok // sum(parts))
    return [(int(a), int(b - a)) for a, b in zip(ends[:-1], ends[1:])]


def tables(blocks, tok, chans, chunks, outs):
    total = 2 * blocks * tok
    freq = np.arange(blocks + 1)
    outer = 2 * np.pi * (freq[:, None] * np.arange(blocks)[None, :] % (2 * blocks)) / (2 * blocks)
    eye = np.eye(chans)
    first = np.concatenate([np.kron(np.cos(outer), eye), np.kron(-np.sin(outer), eye)])
    last = np.concatenate([np.kron(np.cos(outer.T), eye), np.kron(-np.sin(outer.T), eye)], axis=1)
    pos = np.arange(tok)
    inner = 2 * np.pi * (pos[:, None] * pos[None, :] % tok) / tok
    c, s = np.cos(inner), np.sin(inner)
    def order(parts):
        return np.concatenate([np.arange(a, a + n) + i * tok for a, n in parts for i in range(2)])

    forward = np.block([[c, -s], [s, c]])[order(chunks)]
    inverse = np.block([[c, s], [-s, c]])[:, order(outs)]
    twist = 2 * np.pi * (freq[:, None] * pos[None, :]) / total
    twist = np.stack([np.cos(twist), np.sin(twist)])[:, :, None, :]
    return (
        first.astype(bf16),
        (last / total).astype(bf16),
        forward.astype(bf16),
        inverse.astype(bf16),
        twist.astype(np.float32),
    )


def mm(a, b):
    return jnp.dot(a, b, preferred_element_type=f32)


def mm_t(a, b):
    return lax.dot_general(a, b, (((1,), (1,)), ((), ())), preferred_element_type=f32)


def unit(n, flipped=None):
    row = lax.broadcasted_iota(jnp.int32, (n, n), 0)
    col = lax.broadcasted_iota(jnp.int32, (n, n), 1)
    if flipped is not None:
        row = jnp.where(flipped, n - 1 - row, row)
    return jnp.where(row == col, 1.0, 0.0).astype(bf16)


def kernel(
    nz, blocks, tok, chans, chunks, outs,
    tokens_hbm, w_in_hbm, w_out_hbm, spectra_hbm, first_hbm, last_hbm, forward_hbm, inverse_hbm, twist_hbm,
    out_hbm,
    feat, w_in, w_cols, w_relay, spec, first, last, forward, inverse, twist,
    acc, hsend, hrecv, filt, sig, xrecv, tmp, part, q, back, v, y, conv, qt,
    gall, side, stage,
    load_sem, ag_send, ag_recv, x_send, x_recv, r_send, r_recv, w_send, w_recv,
):
    me = lax.axis_index("seq")
    z = lax.axis_index("ch")
    right, left, opp = lax.rem(z + 1, nz), lax.rem(z + nz - 1, nz), lax.rem(z + 2, nz)
    width = chans * blocks
    depth = tokens_hbm.shape[1]

    def load(src, dst, sem):
        return pltpu.make_async_copy(src, dst, load_sem.at[sem])

    def load_w(block, sem):
        at = pl.ds(pl.multiple_of(block * depth, depth), depth)
        return load(w_in_hbm.at[:, at], w_in.at[:, at], sem)

    tok_load = load(tokens_hbm, feat.at[z], 0)
    spec_load = load(spectra_hbm, spec, 1)
    w_loads = [load_w(z, 2), load_w(left, 3), load_w(right, 4), load_w(opp, 5)]
    rest = [
        load(first_hbm, first, 7), load(last_hbm, last, 8),
        load(forward_hbm, forward, 9), load(inverse_hbm, inverse, 10), load(twist_hbm, twist, 11),
    ]
    tok_load.start()
    spec_load.start()
    for copy in w_loads + rest:
        copy.start()

    barrier = pltpu.get_barrier_semaphore()
    for near in (left, right):
        pl.semaphore_signal(barrier, inc=1, device_id=(me, near), device_id_type=MESH)

    def peers(act):
        mid = blocks // 2
        for low, high in ((mid, blocks), (blocks + 1, blocks + mid)):
            @pl.loop(low, high, unroll=True)
            def _(k):
                act(lax.rem(me + k, blocks))

    peers(lambda peer: pl.semaphore_signal(barrier, inc=1, device_id=(peer, z), device_id_type=MESH))
    pl.semaphore_wait(barrier, blocks + 1)
    tok_load.wait()

    core = lax.rem(me, 2)
    sibling = me + 1 - 2 * core
    line = 4 if blocks >= 32 else blocks // 2
    at_x, at_y = lax.rem(me // 2, line), me // (2 * line)
    even_x = 1 - lax.rem(at_x, 2)
    pair_x = me + 4 * even_x - 2
    if blocks >= 32:
        even_y = 1 - lax.rem(at_y, 2)
        pair_y = me + 2 * line * (2 * even_y - 1)
        pair_far = me + 2 * (lax.rem(at_x + line + 1 - 2 * even_x, line) - at_x)
    else:
        even_y, pair_y, pair_far = even_x, pair_x, pair_x
    foreign = (left, right, opp)
    pairs = (pair_x, pair_y, pair_far)
    sides = (even_x, even_y, even_x)
    fourth, eighth = width // 4, width // 8

    def w_rows(c, i, away=0, start=0, count=fourth):
        side = sides[i] if away == 0 else 1 - sides[i]
        return pl.ds(pl.multiple_of((2 * c + side) * fourth, fourth) + start, count)

    def w_give(src, dst, sem, to, line=me):
        return pltpu.make_async_remote_copy(
            src_ref=src, dst_ref=dst, send_sem=w_send.at[sem], recv_sem=w_recv.at[sem],
            device_id=(line, to), device_id_type=MESH,
        )

    def w_slice(rows_at, block):
        return w_out_hbm.at[rows_at, pl.ds(pl.multiple_of(block * depth, depth), depth)]

    def same(ref, sem):
        return w_give(ref, ref, sem, right)

    first_e, second_e = w_rows(core, 2, 0, 0, eighth), w_rows(core, 2, 0, eighth, eighth)
    w_near = [
        w_give(w_slice(first_e, opp), w_relay.at[0], 2, right),
        w_give(w_slice(second_e, opp), w_relay.at[1], 3, left),
        w_give(w_slice(w_rows(core, 0), right), w_cols.at[z, w_rows(core, 0)], 0, right),
        w_give(w_slice(w_rows(core, 1), left), w_cols.at[z, w_rows(core, 1)], 1, left),
    ]
    w_got = [
        same(w_relay.at[0], 2), same(w_relay.at[1], 3),
        same(w_cols.at[left, w_rows(core, 0)], 0), same(w_cols.at[right, w_rows(core, 1)], 1),
    ]
    w_fwd = [
        w_give(w_relay.at[0], w_cols.at[left, first_e], 4, right),
        w_give(w_relay.at[1], w_cols.at[right, second_e], 5, left),
    ]
    w_fwd_got = [same(w_cols.at[opp, first_e], 4), same(w_cols.at[opp, second_e], 5)]

    def w_pairs(away):
        refs = [w_cols.at[foreign[i], w_rows(core, i, away)] for i in range(3)]
        return [w_give(refs[i], refs[i], 6 + i, z, pairs[i]) for i in range(3)]

    def w_shares(c):
        refs = [w_cols.at[block, pl.ds(pl.multiple_of(c * 2 * fourth, fourth), 2 * fourth)] for block in foreign]
        return [w_give(refs[i], refs[i], 9 + i, z, sibling) for i in range(3)]

    w_pair, w_paired = w_pairs(0), w_pairs(1)
    w_share, w_theirs = w_shares(core), w_shares(1 - core)
    own_w = load(w_slice(pl.ds(0, width), z), w_cols.at[z], 6)
    own_w.start()

    def hop(buf, sems, block, at, sem, to):
        return pltpu.make_async_remote_copy(
            src_ref=buf.at[block, at], dst_ref=buf.at[block, at],
            send_sem=sems[0].at[sem], recv_sem=sems[1].at[sem],
            device_id=(me, to), device_id_type=MESH,
        )

    def full(span):
        return pl.ds(*span)

    def upper(span):
        return pl.ds(span[0], span[1] // 2)

    def lower(span):
        return pl.ds(span[0] + span[1] // 2, span[1] // 2)

    class Ring:
        def __init__(self, parts, buf, *sems):
            self.parts, self.buf, self.sems = parts, buf, sems
            self.started = []

        def start(self, *copies):
            for copy in copies:
                copy.start()
                self.started.append(copy)

        def copy(self, *what):
            return hop(self.buf, self.sems, *what)

        def own(self, c):
            self.start(self.copy(z, full(self.parts[c]), 4 * c, right), self.copy(z, full(self.parts[c]), 4 * c + 1, left))

        def near(self, c):
            self.copy(left, full(self.parts[c]), 4 * c, right).wait_recv()
            self.start(self.copy(left, upper(self.parts[c]), 4 * c + 2, right))
            self.copy(right, full(self.parts[c]), 4 * c + 1, left).wait_recv()
            self.start(self.copy(right, lower(self.parts[c]), 4 * c + 3, left))

        def far(self, c):
            self.copy(opp, upper(self.parts[c]), 4 * c + 2, right).wait_recv()
            self.copy(opp, lower(self.parts[c]), 4 * c + 3, left).wait_recv()

        def sent(self):
            for copy in self.started:
                copy.wait_send()

    tokens = Ring(chunks, feat, ag_send, ag_recv)
    for c in range(min(2, len(chunks))):
        tokens.own(c)

    def swap(src, dst, cols, sems, mine, theirs):
        where = () if cols is None else (slice(None), cols)
        return lambda peer: pltpu.make_async_remote_copy(
            src_ref=src.at[(mine, *where)], dst_ref=dst.at[(theirs, *where)],
            send_sem=x_send.at[sems], recv_sem=x_recv.at[sems],
            device_id=(peer, z), device_id_type=MESH,
        )

    def swap_start(src, dst, cols, sems):
        peers(lambda peer: swap(src, dst, cols, sems, peer, me)(peer).start())
        where = () if cols is None else (slice(None), cols)
        dst[(pl.ds(me, 1), *where)] = src[(pl.ds(me, 1), *where)]

    others = pl.ds(0, blocks - 1)

    def swap_arrived(*refs):
        swap(*refs, others, others)(me).wait_recv()

    def swap_sent(*refs):
        swap(*refs, others, others)(me).wait_send()

    h_refs = (hsend, hrecv, None, 0)
    spec_load.wait()
    for a in range(2):
        for ri in range(2):
            turned = mm_t(unit(width), spec[ri, a].astype(bf16)).astype(bf16)
            turned = mm(turned, unit(tok, 2 * me + a > blocks)).astype(bf16)
            hsend[:, ri, a] = turned.reshape(blocks, chans, tok)
    swap_start(*h_refs)

    def project(block, c, low=0, high=3):
        at = pl.ds(pl.multiple_of(block * depth, depth), depth)
        rows_at = full(chunks[c])

        @pl.loop(low, high)
        def _(g):
            acc[g, rows_at] += mm(feat[block, rows_at], w_in[g, at])

    w_loads[0].wait()
    own_at = pl.ds(pl.multiple_of(z * depth, depth), depth)

    @pl.loop(0, 3)
    def _(g):
        acc[g] = mm(feat[z], w_in[g, own_at])

    def s_refs(c):
        return sig, xrecv, full(chunks[c]), 1 + c

    def far_chunk(c):
        tokens.far(c)
        project(opp, c, 1, 3)
        rows_at = full(chunks[c])
        keys, values = acc[1, rows_at].astype(bf16), acc[2, rows_at].astype(bf16)
        signal = (keys.astype(f32) * values.astype(f32)).astype(bf16)
        turned = mm_t(unit(width), signal).astype(bf16)
        sig[:, :, rows_at] = turned.reshape(blocks, chans, chunks[c][1])
        swap_start(*s_refs(c))
        project(opp, c, 0, 1)

    final = len(chunks) - 1
    for c in range(final + 1):
        tokens.near(c)
        if c + 2 <= final:
            tokens.own(c + 2)
        if c == final:
            for copy in w_near:
                copy.start()
        if c == 0:
            w_loads[1].wait()
            w_loads[2].wait()
        project(left, c)
        project(right, c)
        if c == min(1, final):
            w_loads[3].wait()
        if c > 0:
            far_chunk(c - 1)
    far_chunk(final)
    qt[...] = mm_t(unit(width), acc[0].astype(bf16)).astype(bf16)

    swap_arrived(*h_refs)
    filt[:, 0] = hrecv[0, :, 0].astype(f32)
    filt[:, blocks] = hrecv[blocks // 2, :, 0].astype(f32)

    @pl.loop(1, blocks)
    def _(a):
        other = 2 * blocks - a
        near = hrecv[a // 2, :, a % 2].astype(f32)
        far = hrecv[other // 2, :, other % 2].astype(f32)
        filt[0, a] = near[0] + far[0]
        filt[1, a] = near[1] - far[1]

    for copy in rest:
        copy.wait()

    def at(a):
        return pl.ds(pl.multiple_of(a * chans, chans), chans)

    def outer_chunk(c):
        swap_arrived(*s_refs(c))
        start, count = chunks[c]
        cols = full(chunks[c])
        tmp[:, :count] = mm(first[...], xrecv[:, :, cols].reshape(blocks * chans, count))
        real, imag = pl.ds(2 * start, count), pl.ds(2 * start + count, count)

        @pl.loop(0, blocks + 1)
        def _(a):
            pr, pi = tmp[at(a), :count], tmp[at(blocks + 1 + a), :count]
            tc, ts = twist[0, a, :, cols], twist[1, a, :, cols]
            q[at(a), real] = (pr * tc + pi * ts).astype(bf16)
            q[at(a), imag] = (pi * tc - pr * ts).astype(bf16)

    early = 2 * chunks[final][0]
    for c in range(final):
        outer_chunk(c)
    if early:
        for i in range(2):
            part[i] = mm(q[:, :early], forward[:early, i * tok:(i + 1) * tok])
    for i in range(2):
        w_got[i].wait_recv()
        w_fwd[i].start()
    outer_chunk(final)
    for i in range(2):
        term = mm(q[:, early:], forward[early:, i * tok:(i + 1) * tok])
        part[i] = part[i] + term if early else term

    @pl.loop(0, blocks + 1)
    def _(a):
        xr, xi = part[0, at(a)], part[1, at(a)]
        hr, hi = filt[0, a], filt[1, a]
        q[at(a), :tok] = (xr * hr - xi * hi).astype(bf16)
        q[at(a), tok:] = (xr * hi + xi * hr).astype(bf16)

    def c_refs(c):
        return y, conv, full(outs[c]), 1 + len(chunks) + c

    for c, (start, count) in enumerate(outs):
        back[:, :2 * count] = mm(q[...], inverse[:, 2 * start:2 * (start + count)])
        cols = full(outs[c])

        @pl.loop(0, blocks + 1)
        def _(a):
            ur, ui = back[at(a), :count], back[at(a), count:2 * count]
            tc, ts = twist[0, a, :, cols], twist[1, a, :, cols]
            v[at(a), :count] = (ur * tc - ui * ts).astype(bf16)
            v[at(blocks + 1 + a), :count] = (ur * ts + ui * tc).astype(bf16)

        y[:, :, cols] = mm(last[...], v[:, :count]).astype(bf16).reshape(blocks, chans, count)
        swap_start(*c_refs(c))

    for i in range(2):
        w_got[2 + i].wait_recv()
        w_pair[i].start()

    rows_all = Ring(outs, gall, r_send, r_recv)

    def gate(c):
        swap_arrived(*c_refs(c))
        cols, count = full(outs[c]), outs[c][1]
        values = conv[:, :, cols].reshape(width, count).astype(f32)
        gated_t = (qt[:, cols].astype(f32) * values).astype(bf16)
        gall[pl.ds(z, 1), cols] = mm_t(unit(count), gated_t).astype(bf16)[None]
        rows_all.own(c)

    def term(block, c):
        return mm(gall[block, full(outs[c])], w_cols[block])

    ends = len(outs)
    for c in range(ends):
        gate(c)
        if c == 0:
            for got in w_fwd_got:
                got.wait_recv()
            w_pair[2].start()
        else:
            rows_all.near(c - 1)
    for i in range(3):
        w_paired[i].wait_recv()
        w_share[i].start()
    rows_all.near(ends - 1)
    own_w.wait()
    for c in range(ends):
        side[full(outs[c])] = term(z, c)
    w_theirs[0].wait_recv()
    w_theirs[1].wait_recv()
    for c in range(ends):
        side[full(outs[c])] += term(left, c) + term(right, c)
    w_theirs[2].wait_recv()
    outgoing = []
    for c in range(ends):
        rows_all.far(c)
        rows_at = full(outs[c])
        stage[rows_at] = (side[rows_at] + term(opp, c)).astype(bf16)
        outgoing.append(load(stage.at[rows_at], out_hbm.at[rows_at], 12 + c))
        outgoing[-1].start()

    for copy in outgoing:
        copy.wait()
    tokens.sent()
    rows_all.sent()
    for copy in w_near + w_fwd + w_pair + w_share:
        copy.wait_send()
    swap_sent(*h_refs)
    for c in range(final + 1):
        swap_sent(*s_refs(c))
    for c in range(ends):
        swap_sent(*c_refs(c))


def local(nz, blocks, tokens, w_in, w_out, spectra):
    tok, depth = tokens.shape
    width = w_in.shape[2]
    chans = width // blocks
    rows = (blocks + 1) * chans
    chunks, outs = spans(IN_PARTS, tok), spans(OUT_PARTS, tok)
    widest_in, widest_out = max(n for _, n in chunks), max(n for _, n in outs)
    consts = [jnp.asarray(t) for t in tables(blocks, tok, chans, chunks, outs)]
    dma = pltpu.SemaphoreType.DMA
    vmem = pltpu.VMEM
    scratch = [
        vmem((nz, tok, depth), bf16),
        vmem((3, nz * depth, width), bf16),
        vmem((nz, width, depth), bf16),
        vmem((2, width // 8, depth), bf16),
        vmem(spectra.shape, f32),
        *[vmem(t.shape, t.dtype) for t in consts],
        vmem((3, tok, width), f32),
        vmem((blocks, 2, 2, chans, tok), bf16),
        vmem((blocks, 2, 2, chans, tok), bf16),
        vmem((2, blocks + 1, chans, tok), f32),
        vmem((blocks, chans, tok), bf16),
        vmem((blocks, chans, tok), bf16),
        vmem((2 * rows, widest_in), f32),
        vmem((2, rows, tok), f32),
        vmem((rows, 2 * tok), bf16),
        vmem((rows, 2 * widest_out), f32),
        vmem((2 * rows, widest_out), bf16),
        vmem((blocks, chans, tok), bf16),
        vmem((blocks, chans, tok), bf16),
        vmem((width, tok), bf16),
        vmem((nz, tok, width), bf16),
        vmem((tok, depth), f32),
        vmem((tok, depth), bf16),
        dma((12 + len(outs),)),
        dma((4 * len(chunks),)), dma((4 * len(chunks),)),
        dma((1 + len(chunks) + len(outs),)), dma((1 + len(chunks) + len(outs),)),
        dma((4 * len(outs),)), dma((4 * len(outs),)),
        dma((12,)), dma((12,)),
    ]
    return pl.pallas_call(
        functools.partial(kernel, nz, blocks, tok, chans, chunks, outs),
        out_shape=jax.ShapeDtypeStruct((tok, depth), bf16),
        in_specs=[pl.BlockSpec(memory_space=pl.ANY)] * 9,
        out_specs=pl.BlockSpec(memory_space=pl.ANY),
        scratch_shapes=scratch,
        compiler_params=pltpu.CompilerParams(
            collective_id=0, has_side_effects=True, vmem_limit_bytes=62 * 1024 * 1024
        ),
    )(tokens, jnp.swapaxes(w_in, 0, 1), w_out, spectra, *consts)


def solution(mesh):
    in_specs = (P("seq", "ch"), P(None, None, "ch"), P("ch", None), P(None, "seq", None, "ch"))
    body = functools.partial(local, mesh.shape["ch"], mesh.shape["seq"])
    return jax.shard_map(body, mesh=mesh, in_specs=in_specs, out_specs=P("seq", "ch"), check_vma=False)
```

```python
import functools

import numpy as np

import jax
import jax.numpy as jnp
from jax import lax
from jax.experimental import pallas as pl
from jax.experimental.pallas import tpu as pltpu
from jax.sharding import PartitionSpec as P

bf16 = jnp.bfloat16
f32 = jnp.float32
MESH = pl.DeviceIdType.MESH
IN_PARTS = (2, 2)
OUT_PARTS = (1, 1, 2)


def spans(parts, tok):
    ends = np.cumsum((0,) + parts) * (tok // sum(parts))
    return [(int(a), int(b - a)) for a, b in zip(ends[:-1], ends[1:])]


def tables(blocks, tok, chans, chunks, outs):
    total = 2 * blocks * tok
    freq = np.arange(blocks + 1)
    outer = 2 * np.pi * (freq[:, None] * np.arange(blocks)[None, :] % (2 * blocks)) / (2 * blocks)
    eye = np.eye(chans)
    first = np.concatenate([np.kron(np.cos(outer), eye), np.kron(-np.sin(outer), eye)])
    last = np.concatenate([np.kron(np.cos(outer.T), eye), np.kron(-np.sin(outer.T), eye)], axis=1)
    pos = np.arange(tok)
    inner = 2 * np.pi * (pos[:, None] * pos[None, :] % tok) / tok
    c, s = np.cos(inner), np.sin(inner)
    def order(parts):
        return np.concatenate([np.arange(a, a + n) + i * tok for a, n in parts for i in range(2)])

    tiles = order([(i, min(128, tok)) for i in range(0, tok, min(128, tok))])
    forward = np.block([[c, -s], [s, c]])[order(chunks)][:, tiles]
    inverse = np.block([[c, s], [-s, c]])[tiles][:, order(outs)]
    twist = 2 * np.pi * (freq[:, None] * pos[None, :]) / total
    twist = np.stack([np.cos(twist), np.sin(twist)])[:, :, None, :]
    return (
        first.astype(bf16),
        (last / total).astype(bf16),
        forward.astype(bf16),
        inverse.astype(bf16),
        twist.astype(np.float32),
    )


def mm(a, b):
    return jnp.dot(a, b, preferred_element_type=f32)


def mm_t(a, b):
    return lax.dot_general(a, b, (((1,), (1,)), ((), ())), preferred_element_type=f32)


def unit(n, flipped=None):
    row = lax.broadcasted_iota(jnp.int32, (n, n), 0)
    col = lax.broadcasted_iota(jnp.int32, (n, n), 1)
    if flipped is not None:
        row = jnp.where(flipped, n - 1 - row, row)
    return jnp.where(row == col, 1.0, 0.0).astype(bf16)


def kernel(
    nz, blocks, tok, chans, chunks, outs,
    tokens_hbm, w_in_hbm, w_out_hbm, spectra_hbm, first_hbm, last_hbm, forward_hbm, inverse_hbm, twist_hbm,
    out_hbm,
    feat, w_in, w_cols, w_relay, spec, first, last, forward, inverse, twist,
    acc, hsend, hrecv, filt, sig, xrecv, tmp, part, q, spec_prod, back, v, y, conv, qt,
    gall, side, stage, eye,
    load_sem, ag_send, ag_recv, x_send, x_recv, r_send, r_recv, w_send, w_recv,
):
    me = lax.axis_index("seq")
    z = lax.axis_index("ch")
    right, left, opp = lax.rem(z + 1, nz), lax.rem(z + nz - 1, nz), lax.rem(z + 2, nz)
    width = chans * blocks
    depth = tokens_hbm.shape[1]

    barrier = pltpu.get_barrier_semaphore()
    for near in (left, right):
        pl.semaphore_signal(barrier, inc=1, device_id=(me, near), device_id_type=MESH)

    def peers(act):
        mid = blocks // 2
        for low, high in ((mid, blocks), (blocks + 1, blocks + mid)):
            @pl.loop(low, high, unroll=True)
            def _(k):
                act(lax.rem(me + k, blocks))

    peers(lambda peer: pl.semaphore_signal(barrier, inc=1, device_id=(peer, z), device_id_type=MESH))
    def load(src, dst, sem):
        return pltpu.make_async_copy(src, dst, load_sem.at[sem])

    def load_w(block, sem):
        at = pl.ds(pl.multiple_of(block * depth, depth), depth)
        return load(w_in_hbm.at[:, at], w_in.at[:, at], sem)

    tok_load = load(tokens_hbm, feat.at[z], 0)
    spec_load = load(spectra_hbm, spec, 1)
    w_loads = [load_w(z, 2), load_w(left, 3), load_w(right, 4), load_w(opp, 5)]
    rest = [
        load(first_hbm, first, 7), load(last_hbm, last, 8),
        load(forward_hbm, forward, 9), load(inverse_hbm, inverse, 10), load(twist_hbm, twist, 11),
    ]
    tok_load.start()
    spec_load.start()
    for copy in w_loads + rest:
        copy.start()

    eye[...] = unit(max(tok, width))

    def same_size(n):
        return eye[:n, :n]

    pl.semaphore_wait(barrier, blocks + 1)
    tok_load.wait()

    core = lax.rem(me, 2)
    sibling = me + 1 - 2 * core
    line = 4 if blocks >= 32 else blocks // 2
    at_x, at_y = lax.rem(me // 2, line), me // (2 * line)
    even_x = 1 - lax.rem(at_x, 2)
    pair_x = me + 4 * even_x - 2
    if blocks >= 32:
        even_y = 1 - lax.rem(at_y, 2)
        pair_y = me + 2 * line * (2 * even_y - 1)
        pair_far = me + 2 * (lax.rem(at_x + line + 1 - 2 * even_x, line) - at_x)
    else:
        even_y, pair_y, pair_far = even_x, pair_x, pair_x
    foreign = (left, right, opp)
    pairs = (pair_x, pair_y, pair_far)
    sides = (even_x, even_y, even_x)
    fourth, eighth = width // 4, width // 8

    def w_rows(c, i, away=0, start=0, count=fourth):
        side = sides[i] if away == 0 else 1 - sides[i]
        return pl.ds(pl.multiple_of((2 * c + side) * fourth, fourth) + start, count)

    def w_give(src, dst, sem, to, line=me):
        return pltpu.make_async_remote_copy(
            src_ref=src, dst_ref=dst, send_sem=w_send.at[sem], recv_sem=w_recv.at[sem],
            device_id=(line, to), device_id_type=MESH,
        )

    def w_slice(rows_at, block):
        return w_out_hbm.at[rows_at, pl.ds(pl.multiple_of(block * depth, depth), depth)]

    def same(ref, sem):
        return w_give(ref, ref, sem, right)

    first_e, second_e = w_rows(core, 2, 0, 0, eighth), w_rows(core, 2, 0, eighth, eighth)
    w_near = [
        w_give(w_slice(first_e, opp), w_relay.at[0], 2, right),
        w_give(w_slice(second_e, opp), w_relay.at[1], 3, left),
        w_give(w_slice(w_rows(core, 0), right), w_cols.at[z, w_rows(core, 0)], 0, right),
        w_give(w_slice(w_rows(core, 1), left), w_cols.at[z, w_rows(core, 1)], 1, left),
    ]
    w_got = [
        same(w_relay.at[0], 2), same(w_relay.at[1], 3),
        same(w_cols.at[left, w_rows(core, 0)], 0), same(w_cols.at[right, w_rows(core, 1)], 1),
    ]
    w_fwd = [
        w_give(w_relay.at[0], w_cols.at[left, first_e], 4, right),
        w_give(w_relay.at[1], w_cols.at[right, second_e], 5, left),
    ]
    w_fwd_got = [same(w_cols.at[opp, first_e], 4), same(w_cols.at[opp, second_e], 5)]

    def w_pairs(away):
        refs = [w_cols.at[foreign[i], w_rows(core, i, away)] for i in range(3)]
        return [w_give(refs[i], refs[i], 6 + i, z, pairs[i]) for i in range(3)]

    def w_shares(c):
        refs = [w_cols.at[block, pl.ds(pl.multiple_of(c * 2 * fourth, fourth), 2 * fourth)] for block in foreign]
        return [w_give(refs[i], refs[i], 9 + i, z, sibling) for i in range(3)]

    w_pair, w_paired = w_pairs(0), w_pairs(1)
    w_share, w_theirs = w_shares(core), w_shares(1 - core)
    own_w = load(w_slice(pl.ds(0, width), z), w_cols.at[z], 6)
    own_w.start()

    def hop(buf, sems, block, at, sem, to):
        return pltpu.make_async_remote_copy(
            src_ref=buf.at[block, at], dst_ref=buf.at[block, at],
            send_sem=sems[0].at[sem], recv_sem=sems[1].at[sem],
            device_id=(me, to), device_id_type=MESH,
        )

    def full(span):
        return pl.ds(*span)

    def upper(span):
        return pl.ds(span[0], span[1] // 2)

    def lower(span):
        return pl.ds(span[0] + span[1] // 2, span[1] // 2)

    class Ring:
        def __init__(self, parts, buf, *sems):
            self.parts, self.buf, self.sems = parts, buf, sems
            self.started = []

        def start(self, *copies):
            for copy in copies:
                copy.start()
                self.started.append(copy)

        def copy(self, *what):
            return hop(self.buf, self.sems, *what)

        def own(self, c):
            self.start(self.copy(z, full(self.parts[c]), 4 * c, right), self.copy(z, full(self.parts[c]), 4 * c + 1, left))

        def near(self, c):
            self.copy(left, full(self.parts[c]), 4 * c, right).wait_recv()
            self.start(self.copy(left, upper(self.parts[c]), 4 * c + 2, right))
            self.copy(right, full(self.parts[c]), 4 * c + 1, left).wait_recv()
            self.start(self.copy(right, lower(self.parts[c]), 4 * c + 3, left))

        def far(self, c):
            self.copy(opp, upper(self.parts[c]), 4 * c + 2, right).wait_recv()
            self.copy(opp, lower(self.parts[c]), 4 * c + 3, left).wait_recv()

        def sent(self):
            for copy in self.started:
                copy.wait_send()

    tokens = Ring(chunks, feat, ag_send, ag_recv)
    for c in range(min(2, len(chunks))):
        tokens.own(c)

    def swap(src, dst, cols, sems, mine, theirs):
        where = () if cols is None else (slice(None), cols)
        return lambda peer: pltpu.make_async_remote_copy(
            src_ref=src.at[(mine, *where)], dst_ref=dst.at[(theirs, *where)],
            send_sem=x_send.at[sems], recv_sem=x_recv.at[sems],
            device_id=(peer, z), device_id_type=MESH,
        )

    def swap_start(src, dst, cols, sems):
        peers(lambda peer: swap(src, dst, cols, sems, peer, me)(peer).start())
        where = () if cols is None else (slice(None), cols)
        dst[(pl.ds(me, 1), *where)] = src[(pl.ds(me, 1), *where)]

    others = pl.ds(0, blocks - 1)

    def swap_arrived(*refs):
        swap(*refs, others, others)(me).wait_recv()

    def swap_sent(*refs):
        swap(*refs, others, others)(me).wait_send()

    h_refs = (hsend, hrecv, None, 0)
    spec_load.wait()
    for a in range(2):
        for ri in range(2):
            turned = mm_t(same_size(width), spec[ri, a].astype(bf16)).astype(bf16)
            turned = mm(turned, unit(tok, 2 * me + a > blocks)).astype(bf16)
            hsend[:, ri, a] = turned.reshape(blocks, chans, tok)
    swap_start(*h_refs)

    def project(block, c, low=0, high=3):
        at = pl.ds(pl.multiple_of(block * depth, depth), depth)
        rows_at = full(chunks[c])

        @pl.loop(low, high, unroll=True)
        def _(g):
            acc[g, rows_at] += mm(feat[block, rows_at], w_in[g, at])

    w_loads[0].wait()
    own_at = pl.ds(pl.multiple_of(z * depth, depth), depth)

    @pl.loop(0, 3)
    def _(g):
        acc[g] = mm(feat[z], w_in[g, own_at])

    def s_refs(c):
        return sig, xrecv, full(chunks[c]), 1 + c

    def far_chunk(c):
        tokens.far(c)
        project(opp, c, 1, 3)
        rows_at = full(chunks[c])
        keys, values = acc[1, rows_at].astype(bf16), acc[2, rows_at].astype(bf16)
        signal = (keys.astype(f32) * values.astype(f32)).astype(bf16)
        turned = mm_t(same_size(width), signal).astype(bf16)
        sig[:, :, rows_at] = turned.reshape(blocks, chans, chunks[c][1])
        swap_start(*s_refs(c))
        project(opp, c, 0, 1)

    final = len(chunks) - 1
    for c in range(final + 1):
        tokens.near(c)
        if c + 2 <= final:
            tokens.own(c + 2)
        if c == final:
            for copy in w_near:
                copy.start()
        if c == 0:
            w_loads[1].wait()
            w_loads[2].wait()
        project(left, c)
        project(right, c)
        if c == min(1, final):
            w_loads[3].wait()
        if c > 0:
            far_chunk(c - 1)
    far_chunk(final)
    qt[...] = mm_t(same_size(width), acc[0].astype(bf16)).astype(bf16)

    swap_arrived(*h_refs)
    filt[:, 0] = hrecv[0, :, 0].astype(f32)
    filt[:, blocks] = hrecv[blocks // 2, :, 0].astype(f32)

    @pl.loop(1, blocks, unroll=True)
    def _(a):
        other = 2 * blocks - a
        near = hrecv[a // 2, :, a % 2].astype(f32)
        far = hrecv[other // 2, :, other % 2].astype(f32)
        filt[0, a] = near[0] + far[0]
        filt[1, a] = near[1] - far[1]

    for copy in rest:
        copy.wait()

    def at(a):
        return pl.ds(pl.multiple_of(a * chans, chans), chans)

    def outer_chunk(c):
        swap_arrived(*s_refs(c))
        start, count = chunks[c]
        cols = full(chunks[c])
        tmp[:, :count] = mm(first[...], xrecv[:, :, cols].reshape(blocks * chans, count))
        real, imag = pl.ds(2 * start, count), pl.ds(2 * start + count, count)

        @pl.loop(0, blocks + 1, unroll=True)
        def _(a):
            pr, pi = tmp[at(a), :count], tmp[at(blocks + 1 + a), :count]
            tc, ts = twist[0, a, :, cols], twist[1, a, :, cols]
            q[at(a), real] = (pr * tc + pi * ts).astype(bf16)
            q[at(a), imag] = (pi * tc - pr * ts).astype(bf16)

    early = 2 * chunks[final][0]
    for c in range(final):
        outer_chunk(c)
    if early:
        part[...] = mm(q[:, :early], forward[:early])
    for i in range(2):
        w_got[i].wait_recv()
        w_fwd[i].start()
    outer_chunk(final)
    tile = min(128, tok)
    for i in range(0, tok, tile):
        both = pl.ds(2 * i, 2 * tile)
        x = mm(q[:, early:], forward[early:, 2 * i:2 * (i + tile)])
        if early:
            x += part[:, both]
        x = x.reshape(blocks + 1, chans, 2 * tile)
        xr, xi = x[..., :tile], x[..., tile:]
        hr, hi = filt[0, :, :, i:i + tile], filt[1, :, :, i:i + tile]
        prod = jnp.concatenate([xr * hr - xi * hi, xr * hi + xi * hr], axis=2)
        spec_prod[:, both] = prod.astype(bf16).reshape((blocks + 1) * chans, 2 * tile)

    def c_refs(c):
        return y, conv, full(outs[c]), 1 + len(chunks) + c

    for c, (start, count) in enumerate(outs):
        back[:, :2 * count] = mm(spec_prod[...], inverse[:, 2 * start:2 * (start + count)])
        cols = full(outs[c])

        @pl.loop(0, blocks + 1, unroll=True)
        def _(a):
            ur, ui = back[at(a), :count], back[at(a), count:2 * count]
            tc, ts = twist[0, a, :, cols], twist[1, a, :, cols]
            v[at(a), :count] = (ur * tc - ui * ts).astype(bf16)
            v[at(blocks + 1 + a), :count] = (ur * ts + ui * tc).astype(bf16)

        y[:, :, cols] = mm(last[...], v[:, :count]).astype(bf16).reshape(blocks, chans, count)
        swap_start(*c_refs(c))

    for i in range(2):
        w_got[2 + i].wait_recv()
        w_pair[i].start()

    rows_all = Ring(outs, gall, r_send, r_recv)

    def gate(c):
        swap_arrived(*c_refs(c))
        cols, count = full(outs[c]), outs[c][1]
        values = conv[:, :, cols].reshape(width, count).astype(f32)
        gated_t = (qt[:, cols].astype(f32) * values).astype(bf16)
        gall[pl.ds(z, 1), cols] = mm_t(same_size(count), gated_t).astype(bf16)[None]
        rows_all.own(c)

    def term(block, c):
        return mm(gall[block, full(outs[c])], w_cols[block])

    ends = len(outs)
    for c in range(ends):
        gate(c)
        if c == 0:
            for got in w_fwd_got:
                got.wait_recv()
            w_pair[2].start()
        else:
            rows_all.near(c - 1)
    for i in range(3):
        w_paired[i].wait_recv()
        w_share[i].start()
    rows_all.near(ends - 1)
    own_w.wait()
    for c in range(ends):
        side[full(outs[c])] = term(z, c)
    w_theirs[0].wait_recv()
    w_theirs[1].wait_recv()
    for c in range(ends):
        side[full(outs[c])] += term(left, c) + term(right, c)
    w_theirs[2].wait_recv()
    outgoing = []
    for c in range(ends):
        rows_all.far(c)
        rows_at = full(outs[c])
        stage[rows_at] = (side[rows_at] + term(opp, c)).astype(bf16)
        outgoing.append(load(stage.at[rows_at], out_hbm.at[rows_at], 12 + c))
        outgoing[-1].start()

    for copy in outgoing:
        copy.wait()
    tokens.sent()
    rows_all.sent()
    for copy in w_near + w_fwd + w_pair + w_share:
        copy.wait_send()
    swap_sent(*h_refs)
    for c in range(final + 1):
        swap_sent(*s_refs(c))
    for c in range(ends):
        swap_sent(*c_refs(c))


def local(nz, blocks, tokens, w_in, w_out, spectra):
    tok, depth = tokens.shape
    width = w_in.shape[2]
    chans = width // blocks
    rows = (blocks + 1) * chans
    chunks, outs = spans(IN_PARTS, tok), spans(OUT_PARTS, tok)
    widest_in, widest_out = max(n for _, n in chunks), max(n for _, n in outs)
    consts = [jnp.asarray(t) for t in tables(blocks, tok, chans, chunks, outs)]
    dma = pltpu.SemaphoreType.DMA
    vmem = pltpu.VMEM
    scratch = [
        vmem((nz, tok, depth), bf16),
        vmem((3, nz * depth, width), bf16),
        vmem((nz, width, depth), bf16),
        vmem((2, width // 8, depth), bf16),
        vmem(spectra.shape, f32),
        *[vmem(t.shape, t.dtype) for t in consts],
        vmem((3, tok, width), f32),
        vmem((blocks, 2, 2, chans, tok), bf16),
        vmem((blocks, 2, 2, chans, tok), bf16),
        vmem((2, blocks + 1, chans, tok), f32),
        vmem((blocks, chans, tok), bf16),
        vmem((blocks, chans, tok), bf16),
        vmem((2 * rows, widest_in), f32),
        vmem((rows, 2 * tok), f32),
        vmem((rows, 2 * tok), bf16),
        vmem((rows, 2 * tok), bf16),
        vmem((rows, 2 * widest_out), f32),
        vmem((2 * rows, widest_out), bf16),
        vmem((blocks, chans, tok), bf16),
        vmem((blocks, chans, tok), bf16),
        vmem((width, tok), bf16),
        vmem((nz, tok, width), bf16),
        vmem((tok, depth), f32),
        vmem((tok, depth), bf16),
        vmem((max(tok, width),) * 2, bf16),
        dma((12 + len(outs),)),
        dma((4 * len(chunks),)), dma((4 * len(chunks),)),
        dma((1 + len(chunks) + len(outs),)), dma((1 + len(chunks) + len(outs),)),
        dma((4 * len(outs),)), dma((4 * len(outs),)),
        dma((12,)), dma((12,)),
    ]
    return pl.pallas_call(
        functools.partial(kernel, nz, blocks, tok, chans, chunks, outs),
        out_shape=jax.ShapeDtypeStruct((tok, depth), bf16),
        in_specs=[pl.BlockSpec(memory_space=pl.ANY)] * 9,
        out_specs=pl.BlockSpec(memory_space=pl.ANY),
        scratch_shapes=scratch,
        compiler_params=pltpu.CompilerParams(
            collective_id=0, has_side_effects=True, vmem_limit_bytes=62 * 1024 * 1024
        ),
    )(tokens, jnp.swapaxes(w_in, 0, 1), w_out, spectra, *consts)


def solution(mesh):
    in_specs = (P("seq", "ch"), P(None, None, "ch"), P("ch", None), P(None, "seq", None, "ch"))
    body = functools.partial(local, mesh.shape["ch"], mesh.shape["seq"])
    return jax.shard_map(body, mesh=mesh, in_specs=in_specs, out_specs=P("seq", "ch"), check_vma=False)
```

```python
import functools

import numpy as np

import jax
import jax.numpy as jnp
from jax import lax
from jax.experimental import pallas as pl
from jax.experimental.pallas import tpu as pltpu
from jax.sharding import PartitionSpec as P

bf16 = jnp.bfloat16
f32 = jnp.float32
MESH = pl.DeviceIdType.MESH
IN_PARTS = (2, 2)
OUT_PARTS = (1, 1, 2)


def spans(parts, tok):
    ends = np.cumsum((0,) + parts) * (tok // sum(parts))
    return [(int(a), int(b - a)) for a, b in zip(ends[:-1], ends[1:])]


def tables(blocks, tok, chans, chunks, outs):
    total = 2 * blocks * tok
    freq = np.arange(blocks + 1)
    outer = 2 * np.pi * (freq[:, None] * np.arange(blocks)[None, :] % (2 * blocks)) / (2 * blocks)
    eye = np.eye(chans)
    first = np.concatenate([np.kron(np.cos(outer), eye), np.kron(-np.sin(outer), eye)])
    last = np.concatenate([np.kron(np.cos(outer.T), eye), np.kron(-np.sin(outer.T), eye)], axis=1)
    pos = np.arange(tok)
    inner = 2 * np.pi * (pos[:, None] * pos[None, :] % tok) / tok
    c, s = np.cos(inner), np.sin(inner)
    def order(parts):
        return np.concatenate([np.arange(a, a + n) + i * tok for a, n in parts for i in range(2)])

    tiles = order([(i, min(128, tok)) for i in range(0, tok, min(128, tok))])
    forward = np.block([[c, -s], [s, c]])[order(chunks)][:, tiles]
    inverse = np.block([[c, s], [-s, c]])[tiles][:, order(outs)]
    twist = 2 * np.pi * (freq[:, None] * pos[None, :]) / total
    twist = np.stack([np.cos(twist), np.sin(twist)])[:, :, None, :]
    return (
        first.astype(bf16),
        (last / total).astype(bf16),
        forward.astype(bf16),
        inverse.astype(bf16),
        twist.astype(np.float32),
    )


def mm(a, b):
    return jnp.dot(a, b, preferred_element_type=f32)


def mm_t(a, b):
    return lax.dot_general(a, b, (((1,), (1,)), ((), ())), preferred_element_type=f32)


def unit(n, flipped=None):
    row = lax.broadcasted_iota(jnp.int32, (n, n), 0)
    col = lax.broadcasted_iota(jnp.int32, (n, n), 1)
    if flipped is not None:
        row = jnp.where(flipped, n - 1 - row, row)
    return jnp.where(row == col, 1.0, 0.0).astype(bf16)


def kernel(
    nz, blocks, tok, chans, chunks, outs,
    tokens_hbm, w_in_hbm, w_out_hbm, spectra_hbm, first_hbm, last_hbm, forward_hbm, inverse_hbm, twist_hbm,
    out_hbm,
    feat, w_in, w_cols, w_relay, spec, first, last, forward, inverse, twist,
    acc, hsend, hrecv, filt, sig, xrecv, tmp, part, q, spec_prod, back, v, y, conv, qt,
    gall, side, stage, eye,
    load_sem, ag_send, ag_recv, x_send, x_recv, r_send, r_recv, w_send, w_recv,
):
    me = lax.axis_index("seq")
    z = lax.axis_index("ch")
    right, left, opp = lax.rem(z + 1, nz), lax.rem(z + nz - 1, nz), lax.rem(z + 2, nz)
    width = chans * blocks
    depth = tokens_hbm.shape[1]

    barrier = pltpu.get_barrier_semaphore()
    for near in (left, right):
        pl.semaphore_signal(barrier, inc=1, device_id=(me, near), device_id_type=MESH)

    def peers(act):
        mid = blocks // 2
        for low, high in ((mid, blocks), (blocks + 1, blocks + mid)):
            @pl.loop(low, high, unroll=True)
            def _(k):
                act(lax.rem(me + k, blocks))

    peers(lambda peer: pl.semaphore_signal(barrier, inc=1, device_id=(peer, z), device_id_type=MESH))
    def load(src, dst, sem):
        return pltpu.make_async_copy(src, dst, load_sem.at[sem])

    def load_w(block, sem):
        at = pl.ds(pl.multiple_of(block * depth, depth), depth)
        return load(w_in_hbm.at[:, at], w_in.at[:, at], sem)

    tok_load = load(tokens_hbm, feat.at[z], 0)
    spec_load = load(spectra_hbm, spec, 1)
    w_loads = [load_w(z, 2), load_w(left, 3), load_w(right, 4), load_w(opp, 5)]
    rest = [
        load(first_hbm, first, 7), load(last_hbm, last, 8),
        load(forward_hbm, forward, 9), load(inverse_hbm, inverse, 10), load(twist_hbm, twist, 11),
    ]
    tok_load.start()
    spec_load.start()
    for copy in w_loads + rest:
        copy.start()

    eye[...] = unit(max(tok, width))

    def same_size(n):
        return eye[:n, :n]

    def h_refs(a):
        return hsend, hrecv, a, a

    def turn_filter(a):
        for ri in range(2):
            turned = mm_t(same_size(width), spec[ri, a].astype(bf16)).astype(bf16)
            turned = mm(turned, unit(tok, 2 * me + a > blocks)).astype(bf16)
            hsend[:, ri, a] = turned.reshape(blocks, chans, tok)

    spec_load.wait()
    turn_filter(0)
    pl.semaphore_wait(barrier, blocks + 1)
    tok_load.wait()

    core = lax.rem(me, 2)
    sibling = me + 1 - 2 * core
    line = 4 if blocks >= 32 else blocks // 2
    at_x, at_y = lax.rem(me // 2, line), me // (2 * line)
    even_x = 1 - lax.rem(at_x, 2)
    pair_x = me + 4 * even_x - 2
    if blocks >= 32:
        even_y = 1 - lax.rem(at_y, 2)
        pair_y = me + 2 * line * (2 * even_y - 1)
        pair_far = me + 2 * (lax.rem(at_x + line + 1 - 2 * even_x, line) - at_x)
    else:
        even_y, pair_y, pair_far = even_x, pair_x, pair_x
    foreign = (left, right, opp)
    pairs = (pair_x, pair_y, pair_far)
    sides = (even_x, even_y, even_x)
    fourth, eighth = width // 4, width // 8

    def w_rows(c, i, away=0, start=0, count=fourth):
        side = sides[i] if away == 0 else 1 - sides[i]
        return pl.ds(pl.multiple_of((2 * c + side) * fourth, fourth) + start, count)

    def w_give(src, dst, sem, to, line=me):
        return pltpu.make_async_remote_copy(
            src_ref=src, dst_ref=dst, send_sem=w_send.at[sem], recv_sem=w_recv.at[sem],
            device_id=(line, to), device_id_type=MESH,
        )

    def w_slice(rows_at, block):
        return w_out_hbm.at[rows_at, pl.ds(pl.multiple_of(block * depth, depth), depth)]

    def same(ref, sem):
        return w_give(ref, ref, sem, right)

    first_e, second_e = w_rows(core, 2, 0, 0, eighth), w_rows(core, 2, 0, eighth, eighth)
    w_near = [
        w_give(w_slice(first_e, opp), w_relay.at[0], 2, right),
        w_give(w_slice(second_e, opp), w_relay.at[1], 3, left),
        w_give(w_slice(w_rows(core, 0), right), w_cols.at[z, w_rows(core, 0)], 0, right),
        w_give(w_slice(w_rows(core, 1), left), w_cols.at[z, w_rows(core, 1)], 1, left),
    ]
    w_got = [
        same(w_relay.at[0], 2), same(w_relay.at[1], 3),
        same(w_cols.at[left, w_rows(core, 0)], 0), same(w_cols.at[right, w_rows(core, 1)], 1),
    ]
    w_fwd = [
        w_give(w_relay.at[0], w_cols.at[left, first_e], 4, right),
        w_give(w_relay.at[1], w_cols.at[right, second_e], 5, left),
    ]
    w_fwd_got = [same(w_cols.at[opp, first_e], 4), same(w_cols.at[opp, second_e], 5)]

    def w_pairs(away):
        refs = [w_cols.at[foreign[i], w_rows(core, i, away)] for i in range(3)]
        return [w_give(refs[i], refs[i], 6 + i, z, pairs[i]) for i in range(3)]

    def w_shares(c):
        refs = [w_cols.at[block, pl.ds(pl.multiple_of(c * 2 * fourth, fourth), 2 * fourth)] for block in foreign]
        return [w_give(refs[i], refs[i], 9 + i, z, sibling) for i in range(3)]

    w_pair, w_paired = w_pairs(0), w_pairs(1)
    w_share, w_theirs = w_shares(core), w_shares(1 - core)
    own_w = load(w_slice(pl.ds(0, width), z), w_cols.at[z], 6)
    own_w.start()

    def hop(buf, sems, block, at, sem, to):
        return pltpu.make_async_remote_copy(
            src_ref=buf.at[block, at], dst_ref=buf.at[block, at],
            send_sem=sems[0].at[sem], recv_sem=sems[1].at[sem],
            device_id=(me, to), device_id_type=MESH,
        )

    def full(span):
        return pl.ds(*span)

    def upper(span):
        return pl.ds(span[0], span[1] // 2)

    def lower(span):
        return pl.ds(span[0] + span[1] // 2, span[1] // 2)

    class Ring:
        def __init__(self, parts, buf, *sems):
            self.parts, self.buf, self.sems = parts, buf, sems
            self.started = []

        def start(self, *copies):
            for copy in copies:
                copy.start()
                self.started.append(copy)

        def copy(self, *what):
            return hop(self.buf, self.sems, *what)

        def own(self, c):
            self.start(self.copy(z, full(self.parts[c]), 4 * c, right), self.copy(z, full(self.parts[c]), 4 * c + 1, left))

        def near(self, c):
            self.copy(left, full(self.parts[c]), 4 * c, right).wait_recv()
            self.start(self.copy(left, upper(self.parts[c]), 4 * c + 2, right))
            self.copy(right, full(self.parts[c]), 4 * c + 1, left).wait_recv()
            self.start(self.copy(right, lower(self.parts[c]), 4 * c + 3, left))

        def far(self, c):
            self.copy(opp, upper(self.parts[c]), 4 * c + 2, right).wait_recv()
            self.copy(opp, lower(self.parts[c]), 4 * c + 3, left).wait_recv()

        def sent(self):
            for copy in self.started:
                copy.wait_send()

    tokens = Ring(chunks, feat, ag_send, ag_recv)
    for c in range(min(2, len(chunks))):
        tokens.own(c)

    def swap(src, dst, cols, sems, mine, theirs):
        where = (slice(None), cols)
        return lambda peer: pltpu.make_async_remote_copy(
            src_ref=src.at[(mine, *where)], dst_ref=dst.at[(theirs, *where)],
            send_sem=x_send.at[sems], recv_sem=x_recv.at[sems],
            device_id=(peer, z), device_id_type=MESH,
        )

    def swap_start(src, dst, cols, sems):
        peers(lambda peer: swap(src, dst, cols, sems, peer, me)(peer).start())
        where = (slice(None), cols)
        dst[(pl.ds(me, 1), *where)] = src[(pl.ds(me, 1), *where)]

    others = pl.ds(0, blocks - 1)

    def swap_arrived(*refs):
        swap(*refs, others, others)(me).wait_recv()

    def swap_sent(*refs):
        swap(*refs, others, others)(me).wait_send()

    swap_start(*h_refs(0))
    turn_filter(1)
    swap_start(*h_refs(1))

    def project(block, c, low=0, high=3):
        at = pl.ds(pl.multiple_of(block * depth, depth), depth)
        rows_at = full(chunks[c])

        @pl.loop(low, high, unroll=True)
        def _(g):
            acc[g, rows_at] += mm(feat[block, rows_at], w_in[g, at])

    w_loads[0].wait()
    own_at = pl.ds(pl.multiple_of(z * depth, depth), depth)

    @pl.loop(0, 3)
    def _(g):
        acc[g] = mm(feat[z], w_in[g, own_at])

    def s_refs(c):
        return sig, xrecv, full(chunks[c]), 2 + c

    def far_chunk(c):
        tokens.far(c)
        project(opp, c, 1, 3)
        rows_at = full(chunks[c])
        keys, values = acc[1, rows_at].astype(bf16), acc[2, rows_at].astype(bf16)
        signal = (keys.astype(f32) * values.astype(f32)).astype(bf16)
        turned = mm_t(same_size(width), signal).astype(bf16)
        sig[:, :, rows_at] = turned.reshape(blocks, chans, chunks[c][1])
        swap_start(*s_refs(c))
        project(opp, c, 0, 1)

    final = len(chunks) - 1
    for c in range(final + 1):
        tokens.near(c)
        if c + 2 <= final:
            tokens.own(c + 2)
        if c == final:
            for copy in w_near:
                copy.start()
        if c == 0:
            w_loads[1].wait()
            w_loads[2].wait()
        project(left, c)
        project(right, c)
        if c == min(1, final):
            w_loads[3].wait()
        if c > 0:
            far_chunk(c - 1)
    far_chunk(final)
    qt[...] = mm_t(same_size(width), acc[0].astype(bf16)).astype(bf16)

    swap_arrived(*h_refs(0))
    swap_arrived(*h_refs(1))
    filt[:, 0] = hrecv[0, :, 0].astype(f32)
    filt[:, blocks] = hrecv[blocks // 2, :, 0].astype(f32)

    @pl.loop(1, blocks, unroll=True)
    def _(a):
        other = 2 * blocks - a
        near = hrecv[a // 2, :, a % 2].astype(f32)
        far = hrecv[other // 2, :, other % 2].astype(f32)
        filt[0, a] = near[0] + far[0]
        filt[1, a] = near[1] - far[1]

    for copy in rest:
        copy.wait()

    def at(a):
        return pl.ds(pl.multiple_of(a * chans, chans), chans)

    def outer_chunk(c):
        swap_arrived(*s_refs(c))
        start, count = chunks[c]
        cols = full(chunks[c])
        tmp[:, :count] = mm(first[...], xrecv[:, :, cols].reshape(blocks * chans, count))
        real, imag = pl.ds(2 * start, count), pl.ds(2 * start + count, count)

        @pl.loop(0, blocks + 1, unroll=True)
        def _(a):
            pr, pi = tmp[at(a), :count], tmp[at(blocks + 1 + a), :count]
            tc, ts = twist[0, a, :, cols], twist[1, a, :, cols]
            q[at(a), real] = (pr * tc + pi * ts).astype(bf16)
            q[at(a), imag] = (pi * tc - pr * ts).astype(bf16)

    early = 2 * chunks[final][0]
    for c in range(final):
        outer_chunk(c)
    if early:
        part[...] = mm(q[:, :early], forward[:early])
    for i in range(2):
        w_got[i].wait_recv()
        w_fwd[i].start()
    outer_chunk(final)
    tile = min(128, tok)
    for i in range(0, tok, tile):
        both = pl.ds(2 * i, 2 * tile)
        x = mm(q[:, early:], forward[early:, 2 * i:2 * (i + tile)])
        if early:
            x += part[:, both]
        x = x.reshape(blocks + 1, chans, 2 * tile)
        xr, xi = x[..., :tile], x[..., tile:]
        hr, hi = filt[0, :, :, i:i + tile], filt[1, :, :, i:i + tile]
        prod = jnp.concatenate([xr * hr - xi * hi, xr * hi + xi * hr], axis=2)
        spec_prod[:, both] = prod.astype(bf16).reshape((blocks + 1) * chans, 2 * tile)

    def c_refs(c):
        return y, conv, full(outs[c]), 2 + len(chunks) + c

    for c, (start, count) in enumerate(outs):
        back[:, :2 * count] = mm(spec_prod[...], inverse[:, 2 * start:2 * (start + count)])
        cols = full(outs[c])

        @pl.loop(0, blocks + 1, unroll=True)
        def _(a):
            ur, ui = back[at(a), :count], back[at(a), count:2 * count]
            tc, ts = twist[0, a, :, cols], twist[1, a, :, cols]
            v[at(a), :count] = (ur * tc - ui * ts).astype(bf16)
            v[at(blocks + 1 + a), :count] = (ur * ts + ui * tc).astype(bf16)

        y[:, :, cols] = mm(last[...], v[:, :count]).astype(bf16).reshape(blocks, chans, count)
        swap_start(*c_refs(c))

    for i in range(2):
        w_got[2 + i].wait_recv()
        w_pair[i].start()

    rows_all = Ring(outs, gall, r_send, r_recv)

    def gate(c):
        swap_arrived(*c_refs(c))
        cols, count = full(outs[c]), outs[c][1]
        values = conv[:, :, cols].reshape(width, count).astype(f32)
        gated_t = (qt[:, cols].astype(f32) * values).astype(bf16)
        gall[pl.ds(z, 1), cols] = mm_t(same_size(count), gated_t).astype(bf16)[None]
        rows_all.own(c)

    def term(block, c):
        return mm(gall[block, full(outs[c])], w_cols[block])

    ends = len(outs)
    for c in range(ends):
        gate(c)
        if c == 0:
            for got in w_fwd_got:
                got.wait_recv()
            w_pair[2].start()
        else:
            rows_all.near(c - 1)
    for i in range(3):
        w_paired[i].wait_recv()
        w_share[i].start()
    rows_all.near(ends - 1)
    own_w.wait()
    for c in range(ends):
        side[full(outs[c])] = term(z, c)
    w_theirs[0].wait_recv()
    w_theirs[1].wait_recv()
    for c in range(ends):
        side[full(outs[c])] += term(left, c) + term(right, c)
    w_theirs[2].wait_recv()

    tokens.sent()
    for copy in w_near + w_fwd + w_pair + w_share:
        copy.wait_send()
    swap_sent(*h_refs(0))
    swap_sent(*h_refs(1))
    for c in range(final + 1):
        swap_sent(*s_refs(c))
    for c in range(ends):
        swap_sent(*c_refs(c))

    outgoing = []
    for c in range(ends):
        rows_all.far(c)
        rows_at = full(outs[c])
        stage[rows_at] = (side[rows_at] + term(opp, c)).astype(bf16)
        outgoing.append(load(stage.at[rows_at], out_hbm.at[rows_at], 12 + c))
        outgoing[-1].start()

    rows_all.sent()
    for copy in outgoing:
        copy.wait()


def local(nz, blocks, tokens, w_in, w_out, spectra):
    tok, depth = tokens.shape
    width = w_in.shape[2]
    chans = width // blocks
    rows = (blocks + 1) * chans
    chunks, outs = spans(IN_PARTS, tok), spans(OUT_PARTS, tok)
    widest_in, widest_out = max(n for _, n in chunks), max(n for _, n in outs)
    consts = [jnp.asarray(t) for t in tables(blocks, tok, chans, chunks, outs)]
    dma = pltpu.SemaphoreType.DMA
    vmem = pltpu.VMEM
    scratch = [
        vmem((nz, tok, depth), bf16),
        vmem((3, nz * depth, width), bf16),
        vmem((nz, width, depth), bf16),
        vmem((2, width // 8, depth), bf16),
        vmem(spectra.shape, f32),
        *[vmem(t.shape, t.dtype) for t in consts],
        vmem((3, tok, width), f32),
        vmem((blocks, 2, 2, chans, tok), bf16),
        vmem((blocks, 2, 2, chans, tok), bf16),
        vmem((2, blocks + 1, chans, tok), f32),
        vmem((blocks, chans, tok), bf16),
        vmem((blocks, chans, tok), bf16),
        vmem((2 * rows, widest_in), f32),
        vmem((rows, 2 * tok), f32),
        vmem((rows, 2 * tok), bf16),
        vmem((rows, 2 * tok), bf16),
        vmem((rows, 2 * widest_out), f32),
        vmem((2 * rows, widest_out), bf16),
        vmem((blocks, chans, tok), bf16),
        vmem((blocks, chans, tok), bf16),
        vmem((width, tok), bf16),
        vmem((nz, tok, width), bf16),
        vmem((tok, depth), f32),
        vmem((tok, depth), bf16),
        vmem((max(tok, width),) * 2, bf16),
        dma((12 + len(outs),)),
        dma((4 * len(chunks),)), dma((4 * len(chunks),)),
        dma((2 + len(chunks) + len(outs),)), dma((2 + len(chunks) + len(outs),)),
        dma((4 * len(outs),)), dma((4 * len(outs),)),
        dma((12,)), dma((12,)),
    ]
    return pl.pallas_call(
        functools.partial(kernel, nz, blocks, tok, chans, chunks, outs),
        out_shape=jax.ShapeDtypeStruct((tok, depth), bf16),
        in_specs=[pl.BlockSpec(memory_space=pl.ANY)] * 9,
        out_specs=pl.BlockSpec(memory_space=pl.ANY),
        scratch_shapes=scratch,
        compiler_params=pltpu.CompilerParams(
            collective_id=0, has_side_effects=True, vmem_limit_bytes=62 * 1024 * 1024
        ),
    )(tokens, jnp.swapaxes(w_in, 0, 1), w_out, spectra, *consts)


def solution(mesh):
    in_specs = (P("seq", "ch"), P(None, None, "ch"), P("ch", None), P(None, "seq", None, "ch"))
    body = functools.partial(local, mesh.shape["ch"], mesh.shape["seq"])
    return jax.shard_map(body, mesh=mesh, in_specs=in_specs, out_specs=P("seq", "ch"), check_vma=False)
```
